256 devices in a mesh: gy: 32 (over z_hi, y, x), gz: 8 (over z_lo, core).
Axes of the slice: x: 4, y: 4, z: 8 (z_hi: 2, z_lo: 4; z = z_hi * 4 + z_lo), core: 2. Of those that a mesh axis runs over, the one named last changes fastest.
Arguments:
- kspace: float32 [2, 4, 256, 32, 256], P(None, None, 'gy', 'gz'), may hold values from -6 to 6
- cotangent: float32 [2, 4, 256, 32, 256], P(None, None, 'gy', 'gz'), may hold values from -6 to 6
- weight_in: bfloat16 [16, 8, 3, 3, 3], replicated, may hold values from -0.4375 to 0.4375
- weight_out: bfloat16 [8, 16, 3, 3, 3], replicated, may hold values from -0.3125 to 0.3125
- consistency_weight: float32 [1], replicated, may hold values from 0.2 to 1
- sampling_mask: int32 [256, 32], P('gy', 'gz'), may hold values 0 or 1
Outputs:
- grad_kspace: float32 [2, 4, 256, 32, 256], P(None, None, 'gy', 'gz')
- grad_weight_in: float32 [16, 8, 3, 3, 3], replicated
- grad_weight_out: float32 [8, 16, 3, 3, 3], replicated
The draws below stay inside these ranges and needn't reach their ends.
Inputs may be any that keep to these rules, and one draw needn't show every extreme that they name: `sampling_mask`: 1 marks a sampled phase-encode line.
All inputs are finite; a program needn't handle non-finite values. No bound on the sum of `sampling_mask` on one device may be relied on, other than what follows from the above.
Results may differ from the reference program's by a relative error of at most 0.0059.
Values may be sent and summed in bfloat16 or wider, within the bound.
A program may use at most 128 MiB of HBM per device.

```python
import math
import jax
import jax.numpy as jnp
from jax import lax

COILS = 4
CHANS = 16
NX = 256
NY = 256
NZ = 32
VOXELS = 2097152


def with_ends(entries, key, smallest, largest):
    place = [jax.random.randint(jax.random.fold_in(key, axis), (), 0, length) for axis, length in enumerate(entries.shape)]
    longest = entries.shape.index(max(entries.shape))
    next_to = place[:longest] + [(place[longest] + 1) % entries.shape[longest]] + place[longest + 1:]
    return entries.at[tuple(place)].set(smallest).at[tuple(next_to)].set(largest)


def level_of(stream_key, shape, shards, low, top_value):
    level, own = 1.0, jax.random.fold_in(stream_key, 6)
    for dim, blocks in shards:
        steps = jnp.exp(jax.random.uniform(jax.random.fold_in(own, dim), (blocks,), jnp.float32, low / len(shards), top_value / len(shards)))
        level = level * jnp.repeat(steps, shape[dim] // blocks).reshape([-1 if axis == dim else 1 for axis in range(len(shape))])
    return level


def centred(rng, shape, deviation, reach, pieces=(), kind=jnp.bfloat16):
    factor_of = level_of(rng, shape, pieces, -0.22, 0.18) if pieces else 1.0
    result = jax.random.normal(rng, shape, jnp.float32) * deviation * factor_of
    return jnp.minimum(jnp.maximum(result, -reach), reach).astype(kind)


def setup_inputs(seed: int = 0) -> dict:
    streams_of = jax.random.split(jax.random.key(seed), 7)
    return {
        "kspace": centred(streams_of[0], (2, COILS, NY, NZ, NX), 1.0, 6.0, ((2, 32), (3, 8)), jnp.float32),
        "cotangent": centred(streams_of[1], (2, COILS, NY, NZ, NX), 1.0, 6.0, ((2, 32), (3, 8)), jnp.float32),
        "weight_in": centred(streams_of[2], (CHANS, 2 * COILS, 3, 3, 3), (54 * COILS) ** -0.5, 0.4375),
        "weight_out": centred(streams_of[3], (2 * COILS, CHANS, 3, 3, 3), (27 * CHANS) ** -0.5, 0.3125),
        "consistency_weight": jnp.clip(jax.random.uniform(streams_of[4], (1,), jnp.float32, 0.2, 1.0), 0.2, 1.0),
        "sampling_mask": with_ends((jax.random.randint(streams_of[5], (NY, NZ), 0, 3) < 1).astype(jnp.int32), jax.random.fold_in(streams_of[5], 1), 0, 1),
    }


def to_complex(parts):
    return parts[0] + 1j * parts[1]

def to_parts(values):
    return jnp.stack([jnp.real(values), jnp.imag(values)]).astype(jnp.float32)

def rounded(values):
    return lax.optimization_barrier(values.astype(jnp.bfloat16)).astype(jnp.float32)

def convolve(volume, kernel):
    return lax.conv_general_dilated(volume, kernel, (1, 1, 1), ((1, 1), (1, 1), (1, 1)), dimension_numbers=('NCDHW', 'OIDHW', 'NCDHW'), precision=lax.Precision.HIGHEST)

def reference(kspace, cotangent, weight_in, weight_out, consistency_weight, sampling_mask):
    coil_count = kspace.shape[1]
    image_field = to_parts(jnp.fft.ifftn(to_complex(kspace), axes=(1, 2), norm='ortho'))
    image_in = rounded(image_field.reshape(1, 2 * coil_count, NY, NZ, NX))
    kernel_in = weight_in.astype(jnp.float32)
    kernel_out = weight_out.astype(jnp.float32)
    hidden, pull_in = jax.vjp(convolve, image_in, kernel_in)
    active = rounded(jax.nn.silu(hidden))
    back_field = -to_parts(jnp.fft.ifftn(to_complex(cotangent), axes=(1, 2), norm='ortho'))
    back_out = rounded(back_field.reshape(1, 2 * coil_count, NY, NZ, NX))
    unused_output, pull_out = jax.vjp(convolve, active, kernel_out)
    back_active, grad_out = pull_out(back_out)
    gate = jax.nn.sigmoid(hidden)
    back_hidden = rounded(back_active * gate * (1.0 + hidden * (1.0 - gate)))
    back_image, grad_in = pull_in(back_hidden)
    spectrum = to_parts(jnp.fft.fftn(to_complex(back_image.reshape(2, coil_count, NY, NZ, NX)), axes=(1, 2), norm='ortho'))
    mask_field = sampling_mask.astype(jnp.float32)[None, None, :, :, None]
    grad_kspace = cotangent - consistency_weight[0] * mask_field * cotangent + spectrum
    scale = 1.0 / math.sqrt(VOXELS)
    return (grad_kspace, grad_in * scale, grad_out * scale)
```

```python
import functools
import math

import jax
import jax.numpy as jnp
import numpy as np
from jax import lax
from jax.experimental import pallas as pl
from jax.experimental.pallas import tpu as pltpu
from jax.sharding import PartitionSpec as P

BF = jnp.bfloat16
F32 = jnp.float32
NT = (((1,), (1,)), ((), ()))
roll = pltpu.roll


def mm(a, b):
    return jnp.dot(a, b, preferred_element_type=F32)


def mm_nt(a, b):
    return lax.dot_general(a, b, NT, preferred_element_type=F32)


def tables():
    z_l, pc, y_l = np.meshgrid(np.arange(4), np.arange(8), np.arange(8), indexing="ij")
    qy = np.zeros((256, 256), np.float32)
    qy[(y_l * 32 + z_l * 8 + pc).ravel(), (z_l * 64 + pc * 8 + y_l).ravel()] = 1
    m, big = np.meshgrid(np.arange(16), np.arange(16), indexing="ij")
    px = np.zeros((256, 256), np.float32)
    px[(m * 16 + big).ravel(), (16 * big + m).ravel()] = 1
    b, f, h, y = np.meshgrid(np.arange(16), np.arange(2), np.arange(2), np.arange(8), indexing="ij")
    ps = np.zeros((512, 512), np.float32)
    ps[(b * 32 + f * 16 + h * 8 + y).ravel(), (y * 64 + h * 32 + f * 16 + b).ravel()] = 1
    b, h, y = np.meshgrid(np.arange(16), np.arange(2), np.arange(8), indexing="ij")
    pb = np.zeros((256, 256), np.float32)
    pb[(y * 32 + h * 16 + b).ravel(), (b * 16 + h * 8 + y).ravel()] = 1
    ky = (128 * h + 8 * b + y).ravel()
    theta = 2 * np.pi * ((np.arange(256)[:, None] * ky[None, :]) % 256) / 256
    wy = np.concatenate([np.cos(theta), np.sin(theta)], 0) / 16
    j, z_l, c = np.meshgrid(np.arange(8), np.arange(4), np.arange(4), indexing="ij")
    kz = (4 * j + z_l).ravel()
    row = (j * 32 + z_l * 8 + c).ravel()
    col = c.ravel()
    mz = np.zeros((512, 256), np.float64)
    for z in range(32):
        phi = 2 * np.pi * ((kz * z) % 32) / 32
        cs, sn = np.cos(phi) / math.sqrt(32), np.sin(phi) / math.sqrt(32)
        re, im = z * 8 + col, z * 8 + 4 + col
        mz[row, re] = cs
        mz[row + 4, re] = -sn
        mz[row, im] = sn
        mz[row + 4, im] = cs
        mz[256 + row, re] = -sn
        mz[256 + row + 4, re] = -cs
        mz[256 + row, im] = cs
        mz[256 + row + 4, im] = -sn
    out = {"qy": qy, "px": px, "ps": ps, "pb": pb, "wy": wy, "mz": mz, "qyt": qy.T, "pxt": px.T}
    out["wyt"] = np.concatenate([wy[:256].T, wy[256:].T], 1)
    out["mzt"] = np.concatenate([mz[:256].T, mz[256:].T], 1)
    high = {k: v.astype(np.float32).astype(BF) for k, v in out.items()}
    for k in ("wy", "mz"):
        low = (out[k] - high[k].astype(np.float64)).astype(np.float32).astype(BF)
        high[k] = np.stack([high[k], low])
    return high


NAMES = ("qy", "px", "ps", "pb", "wy", "mz", "wyt", "mzt", "qyt", "pxt")


def pack(x, qy, px):
    u = mm(qy, x.astype(BF)).astype(BF)
    return mm_nt(px, u).astype(BF)


def unpack(a, qyt, pxt):
    u = mm(pxt, a).astype(BF)
    return mm_nt(qyt, u)


def swap_blocks(parts):
    parts = list(parts)
    block = lax.broadcasted_iota(jnp.int32, parts[0].shape, 1) // 32
    for bit in (1, 2, 4):
        low = (block & bit) == 0
        for j in range(8):
            if not j & bit:
                a, b = parts[j], parts[j | bit]
                parts[j] = jnp.where(low, a, roll(b, 32 * bit, 1))
                parts[j | bit] = jnp.where(low, roll(a, 256 - 32 * bit, 1), b)
    return parts


def to_volume(d, wy, mz):
    cs = mm(wy[0], d) + mm(wy[1], d)
    cs = jnp.concatenate([cs[:256], cs[256:]], axis=1)
    high = cs.astype(BF)
    low = (cs - high.astype(F32)).astype(BF)
    return mm(high, mz[0]) + (mm(high, mz[1]) + mm(low, mz[0]))


def from_volume(v, wyt, mzt):
    e = mm(v.astype(BF), mzt).astype(BF)
    return mm(wyt, jnp.concatenate([e[:, :256], e[:, 256:]], axis=0)).astype(BF)


def shifted(v, u):
    if u == 0:
        return v
    row = lax.broadcasted_iota(jnp.int32, v.shape, 0)
    n = v.shape[0]
    if u == 1:
        return jnp.where(row == n - 1, 0.0, roll(v, n - 1, 0))
    return jnp.where(row == 0, 0.0, roll(v, 1, 0))


def band_rows(w, pair):
    lane = lax.broadcasted_iota(jnp.int32, (16, 512), 1)
    row = lax.broadcasted_iota(jnp.int32, (16, 512), 0)
    u = 2 * pair + row // 8 - lane // 16
    wide = [jnp.concatenate([k] * 4, axis=1) for k in w]
    zero = jnp.zeros((16, 512), F32)
    return jnp.where(u == -1, wide[0], jnp.where(u == 0, wide[1], jnp.where(u == 1, wide[2], zero)))


def band_sums(g):
    zp = lax.broadcasted_iota(jnp.int32, (16, 256), 1) // 8
    acc = [jnp.zeros((16, 256), F32) for _ in range(3)]
    for z in range(32):
        t = zp - z
        acc[z % 3] = jnp.where((t >= -1) & (t <= 1), g[z * 16:(z + 1) * 16], acc[z % 3])
    out = []
    for u in (-1, 0, 1):
        z = zp - u
        r = (z + 3) % 3
        s = jnp.where(r == 0, acc[0], jnp.where(r == 1, acc[1], acc[2]))
        s = jnp.where((z >= 0) & (z < 32), s, 0.0)
        s = s[:, :128] + s[:, 128:]
        for step in (64, 32, 16, 8):
            s = s + roll(s, step, 1)
        out.append(s)
    return out


def gates(hidden, back_active):
    gate = jax.nn.sigmoid(hidden)
    return hidden * gate, back_active * gate * (1.0 + hidden * (1.0 - gate))


def kernel(kspace, cotangent, factor, wt, qy, px, ps, pb, wy, mz, wyt, mzt, qyt, pxt,
           out, grads,
           a1, r1, s2, r2, plane, halo, fcat, band, zt, bh, send_p, recv_p, s3, r3, s4, r4, gr, ga, gs, gb, gt, gc,
           sem1, sem2, semh, semp, sem3, sem4, semg1, semg2, semg3):
    g = lax.axis_index("gy")
    j = lax.axis_index("gz")
    h, b = g // 16, g % 16
    m = h * 8 + j

    def dev1(p):
        return ((p // 8) * 16 + b, p % 8)

    def dev2(p):
        return (h * 16 + p, j)

    def at_x(p):
        mm_, bb = p % 16, p // 16
        return ((mm_ // 8) * 16 + bb, mm_ % 8)

    x = b * 16 + m
    right = at_x((x + 1) % 256)
    left = at_x((x + 255) % 256)

    barrier = pltpu.get_barrier_semaphore()

    def greet(d, carry):
        pl.semaphore_signal(barrier, inc=1, device_id=dev1((m + d) % 16), device_id_type=pl.DeviceIdType.MESH)
        pl.semaphore_signal(barrier, inc=1, device_id=dev2((b + d) % 16), device_id_type=pl.DeviceIdType.MESH)
        return carry

    lax.fori_loop(1, 16, greet, 0)
    pl.semaphore_signal(barrier, inc=1, device_id=right, device_id_type=pl.DeviceIdType.MESH)
    pl.semaphore_signal(barrier, inc=1, device_id=left, device_id_type=pl.DeviceIdType.MESH)

    def remote(src, dst, sems, i, device):
        return pltpu.make_async_remote_copy(
            src_ref=src, dst_ref=dst, send_sem=sems.at[0, i], recv_sem=sems.at[1, i],
            device_id=device, device_id_type=pl.DeviceIdType.MESH)

    def send_all(me, dev, src, dst, sems):
        def step(d, carry):
            p = (me + d) % 16
            remote(src(p), dst(me), sems, d, dev(p)).start()
            return carry
        lax.fori_loop(1, 16, step, 0)

    def wait_all(me, dev, src, dst, sems):
        def step(d, carry):
            p = (me + d) % 16
            q = (me + 16 - d) % 16
            remote(src(p), dst(q), sems, d, dev(p)).wait_send()
            remote(src(p), dst(q), sems, d, dev(p)).wait_recv()
            return carry
        lax.fori_loop(1, 16, step, 0)

    for f, field in enumerate((kspace, cotangent)):
        rows = jnp.concatenate([field[:, z, :] for z in range(4)], axis=0)
        a1[:, f] = pack(rows, qy[...], px[...]).reshape(16, 16, 256)

    pl.semaphore_wait(barrier, 32)

    ex1 = (m, dev1, lambda p: a1.at[p], lambda p: r1.at[p], sem1)
    send_all(*ex1)
    r1[m] = a1[m]

    def build(t, carry):
        w = [wt[t, u] for u in range(3)]
        for pair in range(16):
            rows_at = pl.multiple_of(t * 256 + pair * 16, 16)
            band[pl.ds(rows_at, 16), :] = band_rows(w, pair).astype(BF)
        return carry

    lax.fori_loop(0, 18, build, 0)
    wait_all(*ex1)

    parts = [jnp.concatenate([r1[k].reshape(32, 256), r1[8 + k].reshape(32, 256)], axis=0).astype(F32) for k in range(8)]
    whole = jnp.concatenate(swap_blocks(parts), axis=0).astype(BF)
    s2[...] = mm(ps[...], whole).astype(BF).reshape(16, 2, 16, 256)
    ex2 = (b, dev2, lambda p: s2.at[p], lambda p: r2.at[:, p], sem2)
    send_all(*ex2)
    r2[:, b] = s2[b]
    wait_all(*ex2)

    for f in range(2):
        v = to_volume(r2[f].reshape(256, 256), wy[...], mz[...])
        plane[f] = (v if f == 0 else -v).astype(BF)

    def halo_copies(f):
        return (remote(plane.at[f], halo.at[0, f], semh, f, right),
                remote(plane.at[f], halo.at[1, f], semh, 2 + f, left))

    for f in range(2):
        for c in halo_copies(f):
            c.start()

    def lay(f, ux, v):
        for uy in (-1, 0, 1):
            tap = (ux + 1) * 3 + uy + 1
            fcat[f, :, tap * 256:(tap + 1) * 256] = shifted(v, uy).astype(BF)

    for f in range(2):
        lay(f, 0, plane[f].astype(F32))
    has_left = jnp.where(x > 0, 1.0, 0.0)
    has_right = jnp.where(x < 255, 1.0, 0.0)
    for f in range(2):
        for c in halo_copies(f):
            c.wait()
        lay(f, -1, halo[0, f].astype(F32) * has_left)
        lay(f, 1, halo[1, f].astype(F32) * has_right)

    hidden = mm(fcat[0], band[0:2304, :])
    back_active = mm(fcat[1], band[2304:4608, :])
    active, back_hidden = gates(hidden, back_active)
    zt[0] = back_hidden.T.astype(BF)
    zt[1] = active.T.astype(BF)
    for uy in (-1, 0, 1):
        bh[uy + 1] = shifted(back_hidden, -uy).astype(BF)

    def share(ux):
        total = None
        for uy in (-1, 0, 1):
            tap = (ux + 1) * 3 + uy + 1
            v = mm_nt(bh[uy + 1], band[tap * 256:(tap + 1) * 256, :])
            total = v if total is None else total + v
        return total

    share_copies = (remote(send_p.at[0], recv_p.at[0], semp, 0, right),
                    remote(send_p.at[1], recv_p.at[1], semp, 1, left))
    send_p[0] = share(1).astype(BF)
    share_copies[0].start()
    send_p[1] = share(-1).astype(BF)
    share_copies[1].start()
    own = share(0)
    for c in share_copies:
        c.wait()
    back_image = own + recv_p[0].astype(F32) * has_left + recv_p[1].astype(F32) * has_right

    s3[...] = from_volume(back_image, wyt[...], mzt[...]).reshape(16, 16, 256)
    ex3 = (b, dev2, lambda p: s3.at[p], lambda p: r3.at[p], sem3)
    send_all(*ex3)
    r3[b] = s3[b]

    gr[...] = jnp.zeros_like(gr)
    slot = lax.broadcasted_iota(jnp.int32, (16, 128), 1) // 8
    for f in range(2):
        for tap in range(9):
            gm = mm(zt[f], fcat[f, :, tap * 256:(tap + 1) * 256])
            for u, s in enumerate(band_sums(gm)):
                k = (f * 9 + tap) * 3 + u
                tile = slice((k // 7) * 16, (k // 7) * 16 + 16)
                gr[tile, :] = jnp.where(slot == k % 7, s, gr[tile, :])
    exg1 = (m, dev1, lambda p: gr.at[pl.ds(pl.multiple_of(p * 8, 8), 8)], lambda p: ga.at[p], semg1)
    send_all(*exg1)
    ga[m] = gr[pl.ds(pl.multiple_of(m * 8, 8), 8), :]

    wait_all(*ex3)
    rows = mm(pb[...], r3[...].reshape(256, 256))
    parts = swap_blocks([rows[k * 32:(k + 1) * 32] for k in range(8)])
    for k in range(8):
        v = parts[k].astype(BF)
        s4[k] = v[:16]
        s4[8 + k] = v[16:]
    ex4 = (m, dev1, lambda p: s4.at[p], lambda p: r4.at[p], sem4)
    send_all(*ex4)
    r4[m] = s4[m]

    wait_all(*exg1)
    gs[...] = jnp.sum(ga[...], axis=0)
    exg2 = (b, dev2, lambda p: gs, lambda p: gb.at[p], semg2)
    send_all(*exg2)
    gb[b] = gs[...]

    wait_all(*ex4)
    spectrum = unpack(r4[...].reshape(256, 256), qyt[...], pxt[...])
    for z in range(4):
        rows = cotangent[:, z, :]
        scaled = rows * factor[z][:, :1]
        out[:, z, :] = rows - scaled + spectrum[z * 64:(z + 1) * 64]

    wait_all(*exg2)
    gt[...] = jnp.sum(gb[...], axis=0)
    exg3 = (m, dev1, lambda p: gt, lambda p: gc.at[p], semg3)
    send_all(*exg3)
    gc[m] = gt[...]
    wait_all(*exg3)
    grads[...] = gc[...]


def local(kspace, cotangent, weight_in, weight_out, consistency_weight, sampling_mask):
    const = tables()
    w_in = weight_in.transpose(4, 2, 3, 1, 0)
    w_out = jnp.flip(weight_out, (2, 3, 4)).transpose(4, 2, 3, 0, 1)
    wt = jnp.stack([w_in, w_out]).reshape(18, 3, 8, 16).astype(F32)
    wt = jnp.tile(wt, (1, 1, 2, 8))
    factor = consistency_weight[0] * sampling_mask.astype(F32)
    factor = jnp.broadcast_to(factor.T[:, None, :, None], (4, 8, 8, 128)).reshape(4, 64, 128)
    vmem = pl.BlockSpec(memory_space=pltpu.VMEM)

    def scratch(*shape, kind=BF):
        return pltpu.VMEM(shape, kind)

    def sems(n):
        return pltpu.SemaphoreType.DMA((2, n))

    out, grads = pl.pallas_call(
        kernel,
        out_shape=(jax.ShapeDtypeStruct((64, 4, 256), F32), jax.ShapeDtypeStruct((16, 8, 128), F32)),
        in_specs=[vmem] * 14,
        out_specs=(vmem, vmem),
        scratch_shapes=[
            scratch(16, 2, 16, 256), scratch(16, 2, 16, 256),
            scratch(16, 2, 16, 256), scratch(2, 16, 16, 256),
            scratch(2, 256, 256), scratch(2, 2, 256, 256),
            scratch(2, 256, 2304), scratch(4608, 512),
            scratch(2, 512, 256), scratch(3, 256, 512),
            scratch(2, 256, 256), scratch(2, 256, 256),
            scratch(16, 16, 256), scratch(16, 16, 256),
            scratch(16, 16, 256), scratch(16, 16, 256),
            scratch(128, 128, kind=F32), scratch(16, 8, 128, kind=F32), scratch(8, 128, kind=F32),
            scratch(16, 8, 128, kind=F32), scratch(8, 128, kind=F32), scratch(16, 8, 128, kind=F32),
            sems(16), sems(16), sems(4), sems(2), sems(16), sems(16), sems(16), sems(16), sems(16),
        ],
        compiler_params=pltpu.CompilerParams(
            collective_id=0, has_side_effects=True, vmem_limit_bytes=48 * 1024 * 1024),
        name="cascade",
    )(kspace.reshape(64, 4, 256), cotangent.reshape(64, 4, 256), factor, wt, *[jnp.asarray(const[k]) for k in NAMES])

    blocks = grads.reshape(8, 16, 16, 8)[:, :, :7].transpose(0, 2, 1, 3).reshape(56, 16, 8)[:54]
    blocks = blocks.reshape(2, 3, 3, 3, 16, 8) * (1.0 / math.sqrt(2097152))
    grad_in = blocks[0].transpose(3, 4, 1, 2, 0)
    grad_out = jnp.flip(blocks[1], (0, 1, 2)).transpose(4, 3, 1, 2, 0)
    return out.reshape(kspace.shape), grad_in, grad_out


def solution(mesh):
    placed = P(None, None, "gy", "gz", None)
    return jax.shard_map(
        local,
        mesh=mesh,
        in_specs=(placed, placed, P(), P(), P(), P("gy", "gz")),
        out_specs=(placed, P(), P()),
        check_vma=False,
    )
```

```python
import math

import jax
import jax.numpy as jnp
import numpy as np
from jax import lax
from jax.experimental import pallas as pl
from jax.experimental.pallas import tpu as pltpu
from jax.sharding import PartitionSpec as P

BF = jnp.bfloat16
F32 = jnp.float32
NT = (((1,), (1,)), ((), ()))
roll = pltpu.roll


def mm(a, b):
    return jnp.dot(a, b, preferred_element_type=F32)


def mm_nt(a, b):
    return lax.dot_general(a, b, NT, preferred_element_type=F32)


def tables():
    z_l, pc, y_l = np.meshgrid(np.arange(4), np.arange(8), np.arange(8), indexing="ij")
    qy = np.zeros((256, 256), np.float32)
    qy[(y_l * 32 + z_l * 8 + pc).ravel(), (z_l * 64 + pc * 8 + y_l).ravel()] = 1
    m, big = np.meshgrid(np.arange(16), np.arange(16), indexing="ij")
    px = np.zeros((256, 256), np.float32)
    px[(m * 16 + big).ravel(), (16 * big + m).ravel()] = 1
    b, h, y = np.meshgrid(np.arange(16), np.arange(2), np.arange(8), indexing="ij")
    pb = np.zeros((256, 256), np.float32)
    pb[(y * 32 + h * 16 + b).ravel(), (b * 16 + h * 8 + y).ravel()] = 1
    ky = (128 * h + 8 * b + y).ravel()
    theta = 2 * np.pi * ((np.arange(256)[:, None] * ky[None, :]) % 256) / 256
    wy = np.concatenate([np.cos(theta), np.sin(theta)], 0) / 16
    j, z_l, c = np.meshgrid(np.arange(8), np.arange(4), np.arange(4), indexing="ij")
    kz = (4 * j + z_l).ravel()
    row = (j * 32 + z_l * 8 + c).ravel()
    col = c.ravel()
    mz = np.zeros((512, 256), np.float64)
    for z in range(32):
        phi = 2 * np.pi * ((kz * z) % 32) / 32
        cs, sn = np.cos(phi) / math.sqrt(32), np.sin(phi) / math.sqrt(32)
        re, im = z * 8 + col, z * 8 + 4 + col
        mz[row, re] = cs
        mz[row + 4, re] = -sn
        mz[row, im] = sn
        mz[row + 4, im] = cs
        mz[256 + row, re] = -sn
        mz[256 + row + 4, re] = -cs
        mz[256 + row, im] = cs
        mz[256 + row + 4, im] = -sn
    out = {"qy": qy, "px": px, "pbt": pb.T, "pb": pb, "wy": wy, "mz": mz, "qyt": qy.T, "pxt": px.T}
    out["wyt"] = np.concatenate([wy[:256].T, wy[256:].T], 1)
    out["mzt"] = np.concatenate([mz[:256].T, mz[256:].T], 1)
    high = {k: v.astype(np.float32).astype(BF) for k, v in out.items()}
    low = {k: (out[k] - high[k].astype(np.float64)).astype(np.float32).astype(BF) for k in ("wy", "mz")}
    first = np.concatenate([high["qy"], high["px"], high["pbt"]])
    wide = np.concatenate([high["wyt"], high["mzt"]])
    rest = np.concatenate([high["wy"], low["wy"], high["mz"], low["mz"], high["pb"], high["qyt"], high["pxt"]])
    return first, wide, rest


def pack(x, qy, px):
    u = mm(qy, x.astype(BF)).astype(BF)
    return mm_nt(px, u).astype(BF)


def unpack(a, qyt, pxt):
    u = mm(pxt, a).astype(BF)
    return mm_nt(qyt, u)


def swap_blocks(parts):
    parts = list(parts)
    block = lax.broadcasted_iota(jnp.int32, parts[0].shape, 1) // 32
    for bit in (1, 2, 4):
        low = (block & bit) == 0
        for j in range(8):
            if not j & bit:
                a, b = parts[j], parts[j | bit]
                parts[j] = jnp.where(low, a, roll(b, 32 * bit, 1))
                parts[j | bit] = jnp.where(low, roll(a, 256 - 32 * bit, 1), b)
    return parts


def to_volume(d, wy, mz):
    cs = mm(wy[0], d) + mm(wy[1], d)
    cs = jnp.concatenate([cs[:256], cs[256:]], axis=1)
    high = cs.astype(BF)
    low = (cs - high.astype(F32)).astype(BF)
    return mm(high, mz[0]) + (mm(high, mz[1]) + mm(low, mz[0]))


def from_volume(v, wyt, mzt):
    e = mm(v.astype(BF), mzt).astype(BF)
    return mm(wyt, jnp.concatenate([e[:, :256], e[:, 256:]], axis=0)).astype(BF)


def shifted(v, u):
    if u == 0:
        return v
    row = lax.broadcasted_iota(jnp.int32, v.shape, 0)
    n = v.shape[0]
    if u == 1:
        return jnp.where(row == n - 1, 0.0, roll(v, n - 1, 0))
    return jnp.where(row == 0, 0.0, roll(v, 1, 0))


def band_block(w, start):
    lane = lax.broadcasted_iota(jnp.int32, (16, 128), 1)
    row = lax.broadcasted_iota(jnp.int32, (16, 128), 0)
    u = row // 8 - start - lane // 16
    return jnp.where(u == -1, w[0], jnp.where(u == 0, w[1], jnp.where(u == 1, w[2], 0.0))).astype(BF)


def band_sums(g):
    zp = lax.broadcasted_iota(jnp.int32, (16, 256), 1) // 8
    acc = [jnp.zeros((16, 256), F32) for _ in range(3)]
    for z in range(32):
        t = zp - z
        acc[z % 3] = jnp.where((t >= -1) & (t <= 1), g[z * 16:(z + 1) * 16], acc[z % 3])
    out = []
    for u in (-1, 0, 1):
        z = zp - u
        r = (z + 3) % 3
        s = jnp.where(r == 0, acc[0], jnp.where(r == 1, acc[1], acc[2]))
        s = jnp.where((z >= 0) & (z < 32), s, 0.0)
        s = s[:, :128] + s[:, 128:]
        for step in (64, 32, 16, 8):
            s = s + roll(s, step, 1)
        out.append(s)
    return out


def gates(hidden, back_active):
    gate = jax.nn.sigmoid(hidden)
    return hidden * gate, back_active * gate * (1.0 + hidden * (1.0 - gate))


def kernel(kspace_hbm, cotangent_hbm, mask, weight_in, weight_out, consistency, first_hbm, wide_hbm, rest_hbm,
           out, grad_in, grad_out,
           kspace, cotangent, first, wide, rest, wt, seml,
           a1, r1, s2, r2, planes, band, zt, bh, send_p, recv_p, s3, r3, s4, r4, gr, ga, gs, gb, gt, gc,
           sem1, sem2, semh, semp, sem3, sem4, semg1, semg2, semg3):
    g = lax.axis_index("gy")
    j = lax.axis_index("gz")
    h, b = g // 16, g % 16
    m = h * 8 + j

    def dev1(p):
        return ((p // 8) * 16 + b, p % 8)

    def dev2(p):
        return (h * 16 + p, j)

    def at_x(p):
        mm_, bb = p % 16, p // 16
        return ((mm_ // 8) * 16 + bb, mm_ % 8)

    x = b * 16 + m
    right = at_x((x + 1) % 256)
    left = at_x((x + 255) % 256)

    barrier = pltpu.get_barrier_semaphore()

    def greet(d, carry):
        pl.semaphore_signal(barrier, inc=1, device_id=dev1((m + d) % 16), device_id_type=pl.DeviceIdType.MESH)
        pl.semaphore_signal(barrier, inc=1, device_id=dev2((b + d) % 16), device_id_type=pl.DeviceIdType.MESH)
        return carry

    lax.fori_loop(1, 16, greet, 0)
    pl.semaphore_signal(barrier, inc=1, device_id=right, device_id_type=pl.DeviceIdType.MESH)
    pl.semaphore_signal(barrier, inc=1, device_id=left, device_id_type=pl.DeviceIdType.MESH)

    loads = [pltpu.make_async_copy(src, dst, seml.at[i]) for i, (src, dst) in enumerate((
        (first_hbm, first), (kspace_hbm, kspace), (cotangent_hbm, cotangent), (rest_hbm, rest), (wide_hbm, wide)))]
    for c in loads:
        c.start()
    qy, px, pbt = (first.at[256 * i:256 * (i + 1)] for i in range(3))
    wyt, mzt = (wide.at[256 * i:256 * (i + 1)] for i in range(2))
    wy, wy_low, mz, mz_low = (rest.at[512 * i:512 * (i + 1)] for i in range(4))
    pb, qyt, pxt = (rest.at[2048 + 256 * i:2304 + 256 * i] for i in range(3))

    def remote(src, dst, sems, i, device):
        return pltpu.make_async_remote_copy(
            src_ref=src, dst_ref=dst, send_sem=sems.at[0, i], recv_sem=sems.at[1, i],
            device_id=device, device_id_type=pl.DeviceIdType.MESH)

    def send_all(me, dev, src, dst, sems):
        def step(d, carry):
            p = (me + d) % 16
            remote(src(p), dst(me), sems, d, dev(p)).start()
            return carry
        lax.fori_loop(1, 16, step, 0)

    def wait_all(me, dev, src, dst, sems):
        def step(d, carry):
            p = (me + d) % 16
            q = (me + 16 - d) % 16
            remote(src(p), dst(q), sems, d, dev(p)).wait_recv()
            remote(src(p), dst(q), sems, d, dev(p)).wait_send()
            return carry
        lax.fori_loop(1, 16, step, 0)

    ex1 = [(m, dev1, lambda p, f=f: a1.at[f, p], lambda p, f=f: r1.at[f, p], sem1.at[f]) for f in range(2)]
    ex2 = [(b, dev2, lambda p, f=f: s2.at[f, p], lambda p, f=f: r2.at[f, p], sem2.at[f]) for f in range(2)]
    loads[0].wait()
    for f, field in enumerate((kspace, cotangent)):
        loads[1 + f].wait()
        rows = jnp.concatenate([field[:, z, :] for z in range(4)], axis=0)
        a1[f] = pack(rows, qy[...], px[...]).reshape(16, 16, 256)
        if f == 0:
            pl.semaphore_wait(barrier, 32)
        send_all(*ex1[f])
        r1[f, m] = a1[f, m]

    spread = (lax.broadcasted_iota(jnp.int32, (16, 128), 1) % 16 == lax.broadcasted_iota(jnp.int32, (16, 128), 0)).astype(BF)
    for f, w in enumerate((weight_in, weight_out)):
        wt[216 * f:216 * (f + 1), :] = mm(w[...].astype(F32).reshape(216, 16).astype(BF), spread)

    def build(t, carry):
        f, uy, ux = t // 9, t % 9 // 3, t % 3
        w = []
        for uz in range(3):
            k = uy * 9 + uz * 3 + ux
            k = k + f * (53 - 2 * k)
            block = wt[pl.ds(pl.multiple_of(k * 8, 8), 8), :]
            w.append(jnp.concatenate([block, block], axis=0))
        at = [band_block(w, -2 * i) for i in range(4)]
        before, after = band_block(w, -8), band_block(w, 2)
        zero = jnp.zeros((16, 128), BF)
        for pair in range(16):
            own = pair // 4
            cells = [zero] * 4
            cells[own] = at[pair % 4]
            if pair % 4 == 0 and own > 0:
                cells[own - 1] = before
            if pair % 4 == 3 and own < 3:
                cells[own + 1] = after
            rows_at = pl.multiple_of(t * 256 + pair * 16, 16)
            band[pl.ds(rows_at, 16), :] = jnp.concatenate(cells, axis=1)
        return carry

    lax.fori_loop(0, 18, build, 0)

    for f in range(2):
        wait_all(*ex1[f])
        parts = [jnp.concatenate([r1[f, k], r1[f, 8 + k]], axis=0).astype(F32) for k in range(8)]
        whole = jnp.concatenate(swap_blocks(parts), axis=0).astype(BF)
        s2[f] = mm(pbt[...], whole).astype(BF).reshape(16, 16, 256)
        send_all(*ex2[f])
        r2[f, b] = s2[f, b]

    def halo_copies(f):
        return (remote(planes.at[f, 1], planes.at[f, 0], semh, f, right),
                remote(planes.at[f, 1], planes.at[f, 2], semh, 2 + f, left))

    loads[3].wait()
    loads[4].wait()
    for f in range(2):
        wait_all(*ex2[f])
        v = to_volume(r2[f].reshape(256, 256), (wy[...], wy_low[...]), (mz[...], mz_low[...]))
        planes[f, 1] = (v if f == 0 else -v).astype(BF)
        for c in halo_copies(f):
            c.start()

    has_left = jnp.where(x > 0, 1.0, 0.0)
    has_right = jnp.where(x < 255, 1.0, 0.0)
    convolved = []
    for f in range(2):
        for c in halo_copies(f):
            c.wait()

        @pl.when(x == 0)
        def _():
            planes[f, 0] = jnp.zeros((256, 256), BF)

        @pl.when(x == 255)
        def _():
            planes[f, 2] = jnp.zeros((256, 256), BF)

        cat = jnp.concatenate([planes[f, ux] for ux in range(3)], axis=1)
        total = None
        for uy in (-1, 0, 1):
            row = f * 2304 + (uy + 1) * 768
            v = shifted(mm(cat, band[row:row + 768, :]), uy)
            total = v if total is None else total + v
        convolved.append(total)

    active, back_hidden = gates(*convolved)
    for uy in (-1, 0, 1):
        bh[uy + 1] = shifted(back_hidden, -uy).astype(BF)

    def share(ux):
        total = None
        for uy in (-1, 0, 1):
            row = (uy + 1) * 768 + (ux + 1) * 256
            v = mm_nt(bh[uy + 1], band[row:row + 256, :])
            total = v if total is None else total + v
        return total

    share_copies = (remote(send_p.at[0], recv_p.at[0], semp, 0, right),
                    remote(send_p.at[1], recv_p.at[1], semp, 1, left))
    send_p[0] = share(1).astype(BF)
    share_copies[0].start()
    send_p[1] = share(-1).astype(BF)
    share_copies[1].start()
    own = share(0)

    lane = lax.broadcasted_iota(jnp.int32, (512, 256), 1)
    for f, v in enumerate((back_hidden, active)):
        v = v.T
        zt[f, 0] = jnp.where(lane == 255, 0.0, roll(v, 255, 1)).astype(BF)
        zt[f, 1] = v.astype(BF)
        zt[f, 2] = jnp.where(lane == 0, 0.0, roll(v, 1, 1)).astype(BF)
    gr[...] = jnp.zeros_like(gr)
    slot = lax.broadcasted_iota(jnp.int32, (16, 128), 1) // 8
    for t in range(18):
        gm = mm(zt[t // 9, t % 9 // 3], planes[t // 9, t % 3])
        for u, s in enumerate(band_sums(gm)):
            k = t * 3 + u
            tile = slice((k // 7) * 16, (k // 7) * 16 + 16)
            gr[tile, :] = jnp.where(slot == k % 7, s, gr[tile, :])
    exg1 = (m, dev1, lambda p: gr.at[pl.ds(pl.multiple_of(p * 8, 8), 8)], lambda p: ga.at[p], semg1)
    send_all(*exg1)
    ga[m] = gr[pl.ds(pl.multiple_of(m * 8, 8), 8), :]

    for c in share_copies:
        c.wait()
    back_image = own + recv_p[0].astype(F32) * has_left + recv_p[1].astype(F32) * has_right

    s3[...] = from_volume(back_image, wyt[...], mzt[...]).reshape(16, 16, 256)
    ex3 = (b, dev2, lambda p: s3.at[p], lambda p: r3.at[p], sem3)
    send_all(*ex3)
    r3[b] = s3[b]

    wait_all(*exg1)
    gs[...] = jnp.sum(ga[...], axis=0)
    exg2 = (b, dev2, lambda p: gs, lambda p: gb.at[p], semg2)
    send_all(*exg2)
    gb[b] = gs[...]

    wait_all(*ex3)
    rows = mm(pb[...], r3[...].reshape(256, 256))
    parts = swap_blocks([rows[k * 32:(k + 1) * 32] for k in range(8)])
    for k in range(8):
        v = parts[k].astype(BF)
        s4[k] = v[:16]
        s4[8 + k] = v[16:]
    ex4 = (m, dev1, lambda p: s4.at[p], lambda p: r4.at[p], sem4)
    send_all(*ex4)
    r4[m] = s4[m]

    wait_all(*exg2)
    gt[...] = jnp.sum(gb[...], axis=0)
    exg3 = (m, dev1, lambda p: gt, lambda p: gc.at[p], semg3)
    send_all(*exg3)
    gc[m] = gt[...]

    wait_all(*ex4)
    spectrum = unpack(r4[...].reshape(256, 256), qyt[...], pxt[...])
    factor = mask[...].astype(F32)
    eye = lax.broadcasted_iota(jnp.int32, (8, 8), 0) == lax.broadcasted_iota(jnp.int32, (8, 8), 1)
    for z in range(4):
        rows = cotangent[:, z, :]
        sampled = jnp.sum(jnp.where(eye, factor[z:z + 1], 0.0), axis=1, keepdims=True) * consistency[0]
        scaled = (rows.reshape(8, 8, 256) * sampled[None]).reshape(64, 256)
        out[:, z, :] = rows - scaled + spectrum[z * 64:(z + 1) * 64]

    wait_all(*exg3)
    turned = gc[...].reshape(128, 128).T
    for t in range(8):
        at_front = turned if t == 0 else roll(turned, 128 - 16 * t, 1)
        for slot_at in range(7):
            k = 7 * t + slot_at
            if k < 54:
                f, uy, ux, uz = k // 27, k // 9 % 3, k // 3 % 3, k % 3
                n = uy * 9 + uz * 3 + ux
                block = at_front[slot_at * 8:slot_at * 8 + 8, :16]
                if f == 0:
                    grad_in[n] = block
                else:
                    grad_out[26 - n] = block


def local(kspace, cotangent, weight_in, weight_out, consistency_weight, sampling_mask):
    w_in = weight_in.transpose(2, 3, 4, 1, 0).reshape(27, 8, 16)
    w_out = weight_out.transpose(2, 3, 4, 0, 1).reshape(27, 8, 16)
    vmem = pl.BlockSpec(memory_space=pltpu.VMEM)
    hbm = pl.BlockSpec(memory_space=pltpu.HBM)

    def scratch(*shape, kind=BF):
        return pltpu.VMEM(shape, kind)

    def sems(n):
        return pltpu.SemaphoreType.DMA((2, n))

    grad_shape = jax.ShapeDtypeStruct((27, 8, 16), F32)
    out, grad_in, grad_out = pl.pallas_call(
        kernel,
        out_shape=(jax.ShapeDtypeStruct((64, 4, 256), F32), grad_shape, grad_shape),
        in_specs=[hbm, hbm, vmem, vmem, vmem, pl.BlockSpec(memory_space=pltpu.SMEM), hbm, hbm, hbm],
        out_specs=(vmem, vmem, vmem),
        scratch_shapes=[
            scratch(64, 4, 256, kind=F32), scratch(64, 4, 256, kind=F32),
            scratch(768, 256), scratch(512, 512), scratch(2816, 256), scratch(432, 128, kind=F32),
            pltpu.SemaphoreType.DMA((5,)),
            scratch(2, 16, 16, 256), scratch(2, 16, 16, 256), scratch(2, 16, 16, 256), scratch(2, 16, 16, 256),
            scratch(2, 3, 256, 256), scratch(4608, 512), scratch(2, 3, 512, 256), scratch(3, 256, 512),
            scratch(2, 256, 256), scratch(2, 256, 256),
            scratch(16, 16, 256), scratch(16, 16, 256),
            scratch(16, 16, 256), scratch(16, 16, 256),
            scratch(128, 128, kind=F32), scratch(16, 8, 128, kind=F32), scratch(8, 128, kind=F32),
            scratch(16, 8, 128, kind=F32), scratch(8, 128, kind=F32), scratch(16, 8, 128, kind=F32),
            pltpu.SemaphoreType.DMA((2, 2, 16)), pltpu.SemaphoreType.DMA((2, 2, 16)), sems(4), sems(2), sems(16), sems(16), sems(16), sems(16), sems(16),
        ],
        compiler_params=pltpu.CompilerParams(
            collective_id=0, has_side_effects=True, vmem_limit_bytes=62 * 1024 * 1024),
        name="cascade",
    )(kspace.reshape(64, 4, 256), cotangent.reshape(64, 4, 256), sampling_mask.T, w_in, w_out, consistency_weight, *map(jnp.asarray, tables()))
    scale = 1.0 / math.sqrt(2097152)
    grad_in = (grad_in * scale).reshape(3, 3, 3, 8, 16).transpose(4, 3, 0, 1, 2)
    grad_out = (grad_out * scale).reshape(3, 3, 3, 8, 16).transpose(3, 4, 0, 1, 2)
    return out.reshape(kspace.shape), grad_in, grad_out


def solution(mesh):
    placed = P(None, None, "gy", "gz", None)
    return jax.shard_map(
        local,
        mesh=mesh,
        in_specs=(placed, placed, P(), P(), P(), P("gy", "gz")),
        out_specs=(placed, P(), P()),
        check_vma=False,
    )
```

```python
import math

import jax
import jax.numpy as jnp
import numpy as np
from jax import lax
from jax.experimental import pallas as pl
from jax.experimental.pallas import tpu as pltpu
from jax.sharding import PartitionSpec as P

BF = jnp.bfloat16
F32 = jnp.float32
NT = (((1,), (1,)), ((), ()))
roll = pltpu.roll


def mm(a, b):
    return jnp.dot(a, b, preferred_element_type=F32)


def mm_nt(a, b):
    return lax.dot_general(a, b, NT, preferred_element_type=F32)


def plane_of(m, b):
    return b * 16 + m


def member_of(x):
    return x % 16, x // 16


def tables():
    z_l, pc, y_l = np.meshgrid(np.arange(4), np.arange(8), np.arange(8), indexing="ij")
    qy = np.zeros((256, 256), np.float32)
    qy[(y_l * 32 + z_l * 8 + pc).ravel(), (z_l * 64 + pc * 8 + y_l).ravel()] = 1
    m, b = np.meshgrid(np.arange(16), np.arange(16), indexing="ij")
    px = np.zeros((256, 256), np.float32)
    px[(m * 16 + b).ravel(), plane_of(m, b).ravel()] = 1
    b, h, y = np.meshgrid(np.arange(16), np.arange(2), np.arange(8), indexing="ij")
    pb = np.zeros((256, 256), np.float32)
    pb[(y * 32 + h * 16 + b).ravel(), (b * 16 + h * 8 + y).ravel()] = 1
    ky = (128 * h + 8 * b + y).ravel()
    theta = 2 * np.pi * ((np.arange(256)[:, None] * ky[None, :]) % 256) / 256
    wy = np.concatenate([np.cos(theta), np.sin(theta)], 0) / 16
    j, z_l, c = np.meshgrid(np.arange(8), np.arange(4), np.arange(4), indexing="ij")
    kz = (4 * j + z_l).ravel()
    row = (j * 32 + z_l * 8 + c).ravel()
    col = c.ravel()
    mz = np.zeros((512, 256), np.float64)
    for z in range(32):
        phi = 2 * np.pi * ((kz * z) % 32) / 32
        cs, sn = np.cos(phi) / math.sqrt(32), np.sin(phi) / math.sqrt(32)
        re, im = z * 8 + col, z * 8 + 4 + col
        mz[row, re] = cs
        mz[row + 4, re] = -sn
        mz[row, im] = sn
        mz[row + 4, im] = cs
        mz[256 + row, re] = -sn
        mz[256 + row + 4, re] = -cs
        mz[256 + row, im] = cs
        mz[256 + row + 4, im] = -sn
    out = {"qy": qy, "px": px, "pbt": pb.T, "pb": pb, "wy": wy, "mz": mz, "qyt": qy.T, "pxt": px.T}
    out["wyt"] = np.concatenate([wy[:256].T, wy[256:].T], 1)
    out["mzt"] = np.concatenate([mz[:256].T, mz[256:].T], 1)
    high = {k: v.astype(np.float32).astype(BF) for k, v in out.items()}
    low = {k: (out[k] - high[k].astype(np.float64)).astype(np.float32).astype(BF) for k in ("wy", "mz")}
    first = np.concatenate([high["qy"], high["px"], high["pbt"]])
    wide = np.concatenate([high["wyt"], high["mzt"]])
    rest = np.concatenate([high["wy"], low["wy"], high["mz"], low["mz"], high["pb"], high["qyt"], high["pxt"]])
    return first, wide, rest


def pack(x, qy, px):
    u = mm(qy, x.astype(BF)).astype(BF)
    return mm_nt(px, u).astype(BF)


def unpack(a, qyt, pxt):
    u = mm(pxt, a).astype(BF)
    return mm_nt(qyt, u)


def swap_four(parts):
    parts = list(parts)
    block = lax.broadcasted_iota(jnp.int32, parts[0].shape, 1) // 32
    for bit in (1, 2):
        low = (block & bit) == 0
        for j in range(4):
            if not j & bit:
                a, b = parts[j], parts[j | bit]
                parts[j] = jnp.where(low, a, roll(b, 32 * bit, 1))
                parts[j | bit] = jnp.where(low, roll(a, 128 - 32 * bit, 1), b)
    return parts


def swap_blocks(parts):
    out = []
    for y in (0, 128):
        low, high = (swap_four([p[:, y:y + 128] for p in parts[k:k + 4]]) for k in (0, 4))
        out += [jnp.concatenate([a, c], axis=1) for a, c in zip(low, high)]
    return out


def to_volume(d, wy, mz):
    cs = mm(wy[0], d) + mm(wy[1], d)
    cs = jnp.concatenate([cs[:256], cs[256:]], axis=1)
    high = cs.astype(BF)
    low = (cs - high.astype(F32)).astype(BF)
    return mm(high, mz[0]) + (mm(high, mz[1]) + mm(low, mz[0]))


def from_volume(v, wyt, mzt):
    e = mm(v.astype(BF), mzt).astype(BF)
    half = e.shape[1] // 2
    return mm(wyt, jnp.concatenate([e[:, :half], e[:, half:]], axis=0)).astype(BF)


def shifted(v, u):
    if u == 0:
        return v
    row = lax.broadcasted_iota(jnp.int32, v.shape, 0)
    n = v.shape[0]
    if u == 1:
        return jnp.where(row == n - 1, 0.0, roll(v, n - 1, 0))
    return jnp.where(row == 0, 0.0, roll(v, 1, 0))


def band_block(w, start):
    lane = lax.broadcasted_iota(jnp.int32, (16, 128), 1)
    row = lax.broadcasted_iota(jnp.int32, (16, 128), 0)
    u = row // 8 - start - lane // 16
    return jnp.where(u == -1, w[0], jnp.where(u == 0, w[1], jnp.where(u == 1, w[2], 0.0))).astype(BF)


def band_sums(g):
    cell = lax.broadcasted_iota(jnp.int32, (16, 128), 1) // 8
    kept = [[jnp.zeros((16, 128), F32) for _ in range(3)] for _ in range(2)]
    for z in range(32):
        for half in range(2):
            if 16 * half - 1 <= z <= 16 * half + 16:
                t = cell + (16 * half - z)
                kept[half][z % 3] = jnp.where(t * t <= 1, g[z * 16:(z + 1) * 16, 128 * half:128 * (half + 1)], kept[half][z % 3])
    out = []
    for u in (-1, 0, 1):
        total = None
        for half in range(2):
            z = cell + (16 * half - u)
            r = (z + 3) % 3
            s = jnp.where(r == 0, kept[half][0], jnp.where(r == 1, kept[half][1], kept[half][2]))
            s = jnp.where((z >= 0) & (z < 32), s, 0.0)
            total = s if total is None else total + s
        out.append(total)
    return out


def lane_sums(v):
    same = (lax.broadcasted_iota(jnp.int32, (128, 128), 0) % 8 == lax.broadcasted_iota(jnp.int32, (128, 128), 1) % 8).astype(BF)
    total = None
    for _ in range(3):
        part = v.astype(BF)
        v = v - part.astype(F32)
        term = mm(part, same)
        total = term if total is None else total + term
    return total


def gates(hidden, back_active):
    gate = jax.nn.sigmoid(hidden)
    return hidden * gate, back_active * gate * (1.0 + hidden * (1.0 - gate))


def kernel(kspace_hbm, cotangent_hbm, mask, weight_in, weight_out, consistency, first_hbm, wide_hbm, rest_hbm,
           out, grad_in, grad_out,
           kspace, cotangent, first, wide, rest, wt, seml,
           a1, r1, s2, r2, planes, band, turned_band, zt, bh, send_p, recv_p, s3, r3, s4, r4, g_lanes, gr, ga, gs, gb, gt, gc,
           sem1, sem2, semh, semp, sem3, sem4, semg1, semg2, semg3):
    g = lax.axis_index("gy")
    j = lax.axis_index("gz")
    h, b = g // 16, g % 16
    m = h * 8 + j

    def dev1(p):
        return (lax.div(p, 8) * 16 + b, lax.rem(p, 8))

    def dev2(p):
        return (h * 16 + p, j)

    def at_x(p):
        member, place = member_of(p)
        return ((member // 8) * 16 + place, member % 8)

    x = plane_of(m, b)
    right = at_x((x + 1) % 256)
    left = at_x((x + 255) % 256)

    barrier = pltpu.get_barrier_semaphore()

    def greet(d, carry):
        pl.semaphore_signal(barrier, inc=1, device_id=dev1((m + d) % 16), device_id_type=pl.DeviceIdType.MESH)
        pl.semaphore_signal(barrier, inc=1, device_id=dev2((b + d) % 16), device_id_type=pl.DeviceIdType.MESH)
        return carry

    lax.fori_loop(1, 16, greet, 0)
    pl.semaphore_signal(barrier, inc=1, device_id=right, device_id_type=pl.DeviceIdType.MESH)
    pl.semaphore_signal(barrier, inc=1, device_id=left, device_id_type=pl.DeviceIdType.MESH)

    loads = [pltpu.make_async_copy(src, dst, seml.at[i]) for i, (src, dst) in enumerate((
        (first_hbm, first), (kspace_hbm, kspace), (cotangent_hbm, cotangent), (rest_hbm, rest), (wide_hbm, wide)))]
    for c in loads:
        c.start()
    qy, px, pbt = (first.at[256 * i:256 * (i + 1)] for i in range(3))
    wyt, mzt = (wide.at[256 * i:256 * (i + 1)] for i in range(2))
    wy, wy_low, mz, mz_low = (rest.at[512 * i:512 * (i + 1)] for i in range(4))
    pb, qyt, pxt = (rest.at[2048 + 256 * i:2304 + 256 * i] for i in range(3))

    def remote(src, dst, sems, i, device):
        return pltpu.make_async_remote_copy(
            src_ref=src, dst_ref=dst, send_sem=sems.at[0, i], recv_sem=sems.at[1, i],
            device_id=device, device_id_type=pl.DeviceIdType.MESH)

    def send_all(me, dev, src, dst, some, sems):
        for d in range(1, 16):
            p = lax.rem(me + d, 16)
            remote(src(p), dst(me), sems, 0, dev(p)).start()

    def wait_all(me, dev, src, dst, some, sems):
        remote(*some, sems, 0, dev(lax.rem(me + 1, 16))).wait_recv()

    def wait_sent(me, dev, src, dst, some, sems):
        remote(*some, sems, 0, dev(lax.rem(me + 1, 16))).wait_send()

    ex1 = [(m, dev1, lambda p, f=f: a1.at[f, p], lambda p, f=f: r1.at[f, p],
            (a1.at[f, 0:15], r1.at[f, 0:15]), sem1.at[f]) for f in range(2)]
    ex2 = [(b, dev2, lambda p, f=f: s2.at[f, p], lambda p, f=f: r2.at[f, p],
            (s2.at[f, 0:15], r2.at[f, 0:15]), sem2.at[f]) for f in range(2)]
    loads[0].wait()
    for f, field in enumerate((kspace, cotangent)):
        loads[1 + f].wait()
        rows = jnp.concatenate([field[:, z, :] for z in range(4)], axis=0)
        a1[f] = pack(rows, qy[...], px[...]).reshape(16, 16, 256)
        if f == 0:
            pl.semaphore_wait(barrier, 32)
        send_all(*ex1[f])
        r1[f, m] = a1[f, m]

    spread = (lax.broadcasted_iota(jnp.int32, (16, 128), 1) % 16 == lax.broadcasted_iota(jnp.int32, (16, 128), 0)).astype(BF)
    for f, w in enumerate((weight_in, weight_out)):
        wt[216 * f:216 * (f + 1), :] = mm(w[...].astype(F32).reshape(216, 16).astype(BF), spread)

    def build(t, carry):
        f, uy, ux = t // 9, t % 9 // 3, t % 3
        w = []
        for uz in range(3):
            k = uy * 9 + uz * 3 + ux
            k = k + f * (53 - 2 * k)
            block = wt[pl.ds(pl.multiple_of(k * 8, 8), 8), :]
            w.append(jnp.concatenate([block, block], axis=0))
        at = [band_block(w, -2 * i) for i in range(4)]
        before, after = band_block(w, -8), band_block(w, 2)
        zero = jnp.zeros((16, 128), BF)
        for pair in range(16):
            own = pair // 4
            cells = [zero] * 4
            cells[own] = at[pair % 4]
            if pair % 4 == 0 and own > 0:
                cells[own - 1] = before
            if pair % 4 == 3 and own < 3:
                cells[own + 1] = after
            rows_at = pl.multiple_of(t * 256 + pair * 16, 16)
            band[pl.ds(rows_at, 16), :] = jnp.concatenate(cells, axis=1)
        return carry

    lax.fori_loop(0, 18, build, 0)

    def turn(t, carry):
        rows_at = pl.multiple_of(t * 256, 256)
        turned_at = pl.multiple_of(t // 3 * 512, 512)
        turned_band[t % 3, pl.ds(turned_at, 512), :] = band[pl.ds(rows_at, 256), :].T
        return carry

    lax.fori_loop(0, 9, turn, 0)

    def halo_copies(f):
        return (remote(planes.at[f, 1], planes.at[f, 0], semh, f, right),
                remote(planes.at[f, 1], planes.at[f, 2], semh, 2 + f, left))

    for f in range(2):
        wait_all(*ex1[f])
        parts = [jnp.concatenate([r1[f, k], r1[f, 8 + k]], axis=0).astype(F32) for k in range(8)]
        whole = jnp.concatenate(swap_blocks(parts), axis=0).astype(BF)
        s2[f] = mm(pbt[...], whole).astype(BF).reshape(16, 16, 256)
        send_all(*ex2[f])
        r2[f, b] = s2[f, b]

    loads[3].wait()
    loads[4].wait()
    for f in range(2):
        wait_sent(*ex1[f])
    for f in range(2):
        wait_all(*ex2[f])
        v = to_volume(r2[f].reshape(256, 256), (wy[...], wy_low[...]), (mz[...], mz_low[...]))
        planes[f, 1] = (v if f == 0 else -v).astype(BF)
        for c in halo_copies(f):
            c.start()

    for f in range(2):
        wait_sent(*ex2[f])
    convolved = []
    for f in range(2):
        for c in halo_copies(f):
            c.wait()

        @pl.when(x == 0)
        def _():
            planes[f, 0] = jnp.zeros((256, 256), BF)

        @pl.when(x == 255)
        def _():
            planes[f, 2] = jnp.zeros((256, 256), BF)

        cat = jnp.concatenate([planes[f, ux] for ux in range(3)], axis=1)
        total = None
        for uy in (-1, 0, 1):
            row = f * 2304 + (uy + 1) * 768
            v = shifted(mm(cat, band[row:row + 768, :]), uy)
            total = v if total is None else total + v
        convolved.append(total)

    active, back_hidden = gates(*convolved)
    for uy in (-1, 0, 1):
        bh[:, (uy + 1) * 512:(uy + 2) * 512] = shifted(back_hidden, -uy).astype(BF)

    def share(side):
        return mm(bh[...], turned_band[side])

    away = x % 2
    near = 1 - away
    share_copies = []
    for i, side in enumerate((away, near)):
        send_p[i] = share(2 * side).astype(BF)
        c = remote(send_p.at[i], recv_p.at[i], semp, i, at_x((x + 255 + 2 * side) % 256))
        c.start()
        share_copies.append(c)
    own = share(1)

    lane = lax.broadcasted_iota(jnp.int32, (512, 256), 1)
    for f, v in enumerate((back_hidden, active)):
        v = v.T
        zt[f, 0] = jnp.where(lane == 255, 0.0, roll(v, 255, 1)).astype(BF)
        zt[f, 1] = v.astype(BF)
        zt[f, 2] = jnp.where(lane == 0, 0.0, roll(v, 1, 1)).astype(BF)
    for t in range(18):
        gm = mm(zt[t // 9, t % 9 // 3], planes[t // 9, t % 3])
        for u, v in enumerate(band_sums(gm)):
            k = t * 3 + u
            g_lanes[k * 16:(k + 1) * 16, :] = v
    sums = lane_sums(g_lanes[...])
    slot = lax.broadcasted_iota(jnp.int32, (16, 128), 1) // 8
    for tile in range(8):
        v = jnp.zeros((16, 128), F32)
        for at in range(7):
            k = 7 * tile + at
            if k < 54:
                v = jnp.where(slot == at, sums[k * 16:(k + 1) * 16], v)
        gr[2 * tile] = v[:8]
        gr[2 * tile + 1] = v[8:]
    exg1 = (m, dev1, lambda p: gr.at[p], lambda p: ga.at[p], (gr.at[0:15], ga.at[0:15]), semg1)
    send_all(*exg1)
    ga[m] = gr[m]

    for c in share_copies:
        c.wait()
    inside = jnp.where((x > 0) & (x < 255), 1.0, 0.0)
    back_image = own + recv_p[0].astype(F32) * inside + recv_p[1].astype(F32)

    s3[...] = from_volume(back_image, wyt[...], mzt[...]).reshape(16, 16, 256)
    ex3 = (b, dev2, lambda p: s3.at[p], lambda p: r3.at[p], (s3.at[0:15], r3.at[0:15]), sem3)
    send_all(*ex3)
    r3[b] = s3[b]

    wait_all(*exg1)
    gs[...] = jnp.broadcast_to(jnp.sum(ga[...], axis=0, keepdims=True), (16, 8, 128))
    exg2 = (b, dev2, lambda p: gs.at[p], lambda p: gb.at[p], (gs.at[0:15], gb.at[0:15]), semg2)
    send_all(*exg2)
    gb[b] = gs[b]

    wait_all(*ex3)
    rows = mm(pb[...], r3[...].reshape(256, 256))
    parts = swap_blocks([rows[k * 32:(k + 1) * 32] for k in range(8)])
    for k in range(8):
        v = parts[k].astype(BF)
        s4[k] = v[:16]
        s4[8 + k] = v[16:]
    ex4 = (m, dev1, lambda p: s4.at[p], lambda p: r4.at[p], (s4.at[0:15], r4.at[0:15]), sem4)
    send_all(*ex4)
    r4[m] = s4[m]

    wait_all(*exg2)
    gt[...] = jnp.broadcast_to(jnp.sum(gb[...], axis=0, keepdims=True), (16, 8, 128))
    exg3 = (m, dev1, lambda p: gt.at[p], lambda p: gc.at[p], (gt.at[0:15], gc.at[0:15]), semg3)
    send_all(*exg3)
    gc[m] = gt[m]

    for e in (ex3, ex4, exg1, exg2, exg3):
        wait_sent(*e)
    wait_all(*ex4)
    spectrum = unpack(r4[...].reshape(256, 256), qyt[...], pxt[...])
    factor = mask[...].astype(F32)
    eye = lax.broadcasted_iota(jnp.int32, (8, 8), 0) == lax.broadcasted_iota(jnp.int32, (8, 8), 1)
    for z in range(4):
        rows = cotangent[:, z, :]
        sampled = jnp.sum(jnp.where(eye, factor[z:z + 1], 0.0), axis=1, keepdims=True) * consistency[0]
        scaled = (rows.reshape(8, 8, 256) * sampled[None]).reshape(64, 256)
        out[:, z, :] = rows - scaled + spectrum[z * 64:(z + 1) * 64]

    wait_all(*exg3)
    turned = gc[...].reshape(128, 128).T
    for t in range(8):
        at_front = turned if t == 0 else roll(turned, 128 - 16 * t, 1)
        for slot_at in range(7):
            k = 7 * t + slot_at
            if k < 54:
                f, uy, ux, uz = k // 27, k // 9 % 3, k // 3 % 3, k % 3
                n = uy * 9 + uz * 3 + ux
                block = at_front[slot_at * 8:slot_at * 8 + 8, :16]
                if f == 0:
                    grad_in[n] = block
                else:
                    grad_out[26 - n] = block


def local(kspace, cotangent, weight_in, weight_out, consistency_weight, sampling_mask):
    w_in = weight_in.transpose(2, 3, 4, 1, 0).reshape(27, 8, 16)
    w_out = weight_out.transpose(2, 3, 4, 0, 1).reshape(27, 8, 16)
    vmem = pl.BlockSpec(memory_space=pltpu.VMEM)
    hbm = pl.BlockSpec(memory_space=pltpu.HBM)

    def scratch(*shape, kind=BF):
        return pltpu.VMEM(shape, kind)

    def sems(n):
        return pltpu.SemaphoreType.DMA((2, n))

    grad_shape = jax.ShapeDtypeStruct((27, 8, 16), F32)
    out, grad_in, grad_out = pl.pallas_call(
        kernel,
        out_shape=(jax.ShapeDtypeStruct((64, 4, 256), F32), grad_shape, grad_shape),
        in_specs=[hbm, hbm, vmem, vmem, vmem, pl.BlockSpec(memory_space=pltpu.SMEM), hbm, hbm, hbm],
        out_specs=(vmem, vmem, vmem),
        scratch_shapes=[
            scratch(64, 4, 256, kind=F32), scratch(64, 4, 256, kind=F32),
            scratch(768, 256), scratch(512, 512), scratch(2816, 256), scratch(432, 128, kind=F32),
            pltpu.SemaphoreType.DMA((5,)),
            scratch(2, 16, 16, 256), scratch(2, 16, 16, 256), scratch(2, 16, 16, 256), scratch(2, 16, 16, 256),
            scratch(2, 3, 256, 256), scratch(4608, 512), scratch(3, 1536, 256), scratch(2, 3, 512, 256), scratch(256, 1536),
            scratch(2, 256, 256), scratch(2, 256, 256),
            scratch(16, 16, 256), scratch(16, 16, 256),
            scratch(16, 16, 256), scratch(16, 16, 256),
            scratch(864, 128, kind=F32), *[scratch(16, 8, 128, kind=F32) for _ in range(6)],
            pltpu.SemaphoreType.DMA((2, 2, 1)), pltpu.SemaphoreType.DMA((2, 2, 1)), sems(4), sems(2), sems(1), sems(1), sems(1), sems(1), sems(1),
        ],
        compiler_params=pltpu.CompilerParams(
            collective_id=0, has_side_effects=True, vmem_limit_bytes=62 * 1024 * 1024),
        name="cascade",
    )(kspace.reshape(64, 4, 256), cotangent.reshape(64, 4, 256), sampling_mask.T, w_in, w_out, consistency_weight, *map(jnp.asarray, tables()))
    scale = 1.0 / math.sqrt(2097152)
    grad_in = (grad_in * scale).reshape(3, 3, 3, 8, 16).transpose(4, 3, 0, 1, 2)
    grad_out = (grad_out * scale).reshape(3, 3, 3, 8, 16).transpose(3, 4, 0, 1, 2)
    return out.reshape(kspace.shape), grad_in, grad_out


def solution(mesh):
    placed = P(None, None, "gy", "gz", None)
    return jax.shard_map(
        local,
        mesh=mesh,
        in_specs=(placed, placed, P(), P(), P(), P("gy", "gz")),
        out_specs=(placed, P(), P()),
        check_vma=False,
    )
```

```python
import math

import jax
import jax.numpy as jnp
import numpy as np
from jax import lax
from jax.experimental import pallas as pl
from jax.experimental.pallas import tpu as pltpu
from jax.sharding import PartitionSpec as P

BF = jnp.bfloat16
F32 = jnp.float32
NT = (((1,), (1,)), ((), ()))
roll = pltpu.roll


def mm(a, b):
    return jnp.dot(a, b, preferred_element_type=F32)


def mm_nt(a, b):
    return lax.dot_general(a, b, NT, preferred_element_type=F32)


def plane_of(m, b):
    return b * 16 + m


def member_of(x):
    return x % 16, x // 16


def tables():
    z_l, pc, y_l = np.meshgrid(np.arange(4), np.arange(8), np.arange(8), indexing="ij")
    qy = np.zeros((256, 256), np.float32)
    qy[(y_l * 32 + z_l * 8 + pc).ravel(), (z_l * 64 + pc * 8 + y_l).ravel()] = 1
    m, b = np.meshgrid(np.arange(16), np.arange(16), indexing="ij")
    px = np.zeros((256, 256), np.float32)
    px[(m * 16 + b).ravel(), plane_of(m, b).ravel()] = 1
    b, h, y = np.meshgrid(np.arange(16), np.arange(2), np.arange(8), indexing="ij")
    pb = np.zeros((256, 256), np.float32)
    pb[(y * 32 + h * 16 + b).ravel(), (b * 16 + h * 8 + y).ravel()] = 1
    ky = (128 * h + 8 * b + y).ravel()
    theta = 2 * np.pi * ((np.arange(256)[:, None] * ky[None, :]) % 256) / 256
    wy = np.concatenate([np.cos(theta), np.sin(theta)], 0) / 16
    j, z_l, c = np.meshgrid(np.arange(8), np.arange(4), np.arange(4), indexing="ij")
    kz = (4 * j + z_l).ravel()
    row = (j * 32 + z_l * 8 + c).ravel()
    col = c.ravel()
    mz = np.zeros((512, 256), np.float64)
    for z in range(32):
        phi = 2 * np.pi * ((kz * z) % 32) / 32
        cs, sn = np.cos(phi) / math.sqrt(32), np.sin(phi) / math.sqrt(32)
        re, im = z * 8 + col, z * 8 + 4 + col
        mz[row, re] = cs
        mz[row + 4, re] = -sn
        mz[row, im] = sn
        mz[row + 4, im] = cs
        mz[256 + row, re] = -sn
        mz[256 + row + 4, re] = -cs
        mz[256 + row, im] = cs
        mz[256 + row + 4, im] = -sn
    out = {"qy": qy, "px": px, "pbt": pb.T, "pb": pb, "wy": wy, "mz": mz, "qyt": qy.T, "pxt": px.T}
    out["wyt"] = np.concatenate([wy[:256].T, wy[256:].T], 1)
    out["mzt"] = np.concatenate([mz[:256].T, mz[256:].T], 1)
    high = {k: v.astype(np.float32).astype(BF) for k, v in out.items()}
    low = {k: (out[k] - high[k].astype(np.float64)).astype(np.float32).astype(BF) for k in ("wy", "mz")}
    first = np.concatenate([high["qy"], high["px"], high["pbt"]])
    wide = np.concatenate([high["wyt"], high["mzt"]])
    rest = np.concatenate([high["wy"], low["wy"], high["mz"], low["mz"], high["pb"], high["qyt"], high["pxt"]])
    return first, wide, rest


def pack(x, qy, px):
    u = mm(qy, x.astype(BF)).astype(BF)
    return mm_nt(px, u).astype(BF)


def unpack(a, qyt, pxt):
    u = mm(pxt, a).astype(BF)
    return mm_nt(qyt, u)


def swap_four(parts):
    parts = list(parts)
    block = lax.broadcasted_iota(jnp.int32, parts[0].shape, 1) // 32
    for bit in (1, 2):
        low = (block & bit) == 0
        for j in range(4):
            if not j & bit:
                a, b = parts[j], parts[j | bit]
                parts[j] = jnp.where(low, a, roll(b, 32 * bit, 1))
                parts[j | bit] = jnp.where(low, roll(a, 128 - 32 * bit, 1), b)
    return parts


def swap_blocks(parts):
    out = []
    for y in (0, 128):
        low, high = (swap_four([p[:, y:y + 128] for p in parts[k:k + 4]]) for k in (0, 4))
        out += [jnp.concatenate([a, c], axis=1) for a, c in zip(low, high)]
    return out


def to_volume(d, wy, mz):
    cs = mm(wy[0], d) + mm(wy[1], d)
    cs = jnp.concatenate([cs[:256], cs[256:]], axis=1)
    high = cs.astype(BF)
    low = (cs - high.astype(F32)).astype(BF)
    return mm(high, mz[0]) + (mm(high, mz[1]) + mm(low, mz[0]))


def from_volume(v, wyt, mzt):
    e = mm(v.astype(BF), mzt).astype(BF)
    half = e.shape[1] // 2
    return mm(wyt, jnp.concatenate([e[:, :half], e[:, half:]], axis=0)).astype(BF)


def shifted(v, u):
    if u == 0:
        return v
    row = lax.broadcasted_iota(jnp.int32, v.shape, 0)
    n = v.shape[0]
    if u == 1:
        return jnp.where(row == n - 1, 0.0, roll(v, n - 1, 0))
    return jnp.where(row == 0, 0.0, roll(v, 1, 0))


def band_block(w, start):
    lane = lax.broadcasted_iota(jnp.int32, (16, 128), 1)
    row = lax.broadcasted_iota(jnp.int32, (16, 128), 0)
    u = row // 8 - start - lane // 16
    return jnp.where(u == -1, w[0], jnp.where(u == 0, w[1], jnp.where(u == 1, w[2], 0.0))).astype(BF)


def band_sums(g):
    cell = lax.broadcasted_iota(jnp.int32, (16, 128), 1) // 8
    kept = [[jnp.zeros((16, 128), F32) for _ in range(3)] for _ in range(2)]
    for z in range(32):
        for half in range(2):
            if 16 * half - 1 <= z <= 16 * half + 16:
                t = cell + (16 * half - z)
                kept[half][z % 3] = jnp.where(t * t <= 1, g[z * 16:(z + 1) * 16, 128 * half:128 * (half + 1)], kept[half][z % 3])
    out = []
    for u in (-1, 0, 1):
        total = None
        for half in range(2):
            z = cell + (16 * half - u)
            r = (z + 3) % 3
            s = jnp.where(r == 0, kept[half][0], jnp.where(r == 1, kept[half][1], kept[half][2]))
            s = jnp.where((z >= 0) & (z < 32), s, 0.0)
            total = s if total is None else total + s
        out.append(total)
    return out


def lane_sums(v):
    same = (lax.broadcasted_iota(jnp.int32, (128, 128), 0) % 8 == lax.broadcasted_iota(jnp.int32, (128, 128), 1) % 8).astype(BF)
    total = None
    for _ in range(3):
        part = v.astype(BF)
        v = v - part.astype(F32)
        term = mm(part, same)
        total = term if total is None else total + term
    return total


def gates(hidden, back_active):
    gate = jax.nn.sigmoid(hidden)
    return hidden * gate, back_active * gate * (1.0 + hidden * (1.0 - gate))


def kernel(kspace_hbm, cotangent_hbm, mask, weight_in, weight_out, consistency, first_hbm, wide_hbm, rest_hbm,
           out, grad_in, grad_out,
           kspace, cotangent, first, wide, rest, wt, seml,
           a1, r1, s2, r2, planes, band, turned_band, zt, bh, send_p, recv_p, s3, r3, s4, r4, g_lanes, gr, ga, gs, gb, gt, gc,
           sem1, sem2, semh, semp, sem3, sem4, semg1, semg2, semg3):
    g = lax.axis_index("gy")
    j = lax.axis_index("gz")
    h, b = g // 16, g % 16
    m = h * 8 + j

    def dev1(p):
        return (lax.div(p, 8) * 16 + b, lax.rem(p, 8))

    def dev2(p):
        return (h * 16 + p, j)

    def at_x(p):
        member, place = member_of(p)
        return ((member // 8) * 16 + place, member % 8)

    x = plane_of(m, b)
    right = at_x((x + 1) % 256)
    left = at_x((x + 255) % 256)

    barrier = pltpu.get_barrier_semaphore()

    def greet(d, carry):
        pl.semaphore_signal(barrier, inc=1, device_id=dev1((m + d) % 16), device_id_type=pl.DeviceIdType.MESH)
        pl.semaphore_signal(barrier, inc=1, device_id=dev2((b + d) % 16), device_id_type=pl.DeviceIdType.MESH)
        return carry

    lax.fori_loop(1, 16, greet, 0)
    pl.semaphore_signal(barrier, inc=1, device_id=right, device_id_type=pl.DeviceIdType.MESH)
    pl.semaphore_signal(barrier, inc=1, device_id=left, device_id_type=pl.DeviceIdType.MESH)

    loads = [pltpu.make_async_copy(src, dst, seml.at[i]) for i, (src, dst) in enumerate((
        (first_hbm, first), (kspace_hbm, kspace), (cotangent_hbm, cotangent), (rest_hbm, rest), (wide_hbm, wide)))]
    for c in loads:
        c.start()
    qy, px, pbt = (first.at[256 * i:256 * (i + 1)] for i in range(3))
    wyt, mzt = (wide.at[256 * i:256 * (i + 1)] for i in range(2))
    wy, wy_low, mz, mz_low = (rest.at[512 * i:512 * (i + 1)] for i in range(4))
    pb, qyt, pxt = (rest.at[2048 + 256 * i:2304 + 256 * i] for i in range(3))

    def remote(src, dst, sems, i, device):
        return pltpu.make_async_remote_copy(
            src_ref=src, dst_ref=dst, send_sem=sems.at[0, i], recv_sem=sems.at[1, i],
            device_id=device, device_id_type=pl.DeviceIdType.MESH)

    def send_all(me, dev, src, dst, some, sems):
        for d in range(1, 16):
            p = lax.rem(me + d, 16)
            remote(src(p), dst(me), sems, 0, dev(p)).start()

    def wait_all(me, dev, src, dst, some, sems):
        remote(*some, sems, 0, dev(lax.rem(me + 1, 16))).wait_recv()

    def wait_sent(me, dev, src, dst, some, sems):
        remote(*some, sems, 0, dev(lax.rem(me + 1, 16))).wait_send()

    ex1 = [(m, dev1, lambda p, f=f: a1.at[f, p], lambda p, f=f: r1.at[f, p],
            (a1.at[f, 0:15], r1.at[f, 0:15]), sem1.at[f]) for f in range(2)]
    ex2 = [(b, dev2, lambda p, f=f: s2.at[f, p], lambda p, f=f: r2.at[f, p],
            (s2.at[f, 0:15], r2.at[f, 0:15]), sem2.at[f]) for f in range(2)]
    loads[0].wait()
    for f, field in enumerate((kspace, cotangent)):
        loads[1 + f].wait()
        rows = jnp.concatenate([field[:, z, :] for z in range(4)], axis=0)
        a1[f] = pack(rows, qy[...], px[...]).reshape(16, 16, 256)
        if f == 0:
            pl.semaphore_wait(barrier, 32)
        send_all(*ex1[f])
        r1[f, m] = a1[f, m]

    spread = (lax.broadcasted_iota(jnp.int32, (16, 128), 1) % 16 == lax.broadcasted_iota(jnp.int32, (16, 128), 0)).astype(BF)
    for f, w in enumerate((weight_in, weight_out)):
        wt[216 * f:216 * (f + 1), :] = mm(w[...].astype(F32).reshape(216, 16).astype(BF), spread)

    def build(t, carry):
        f, uy, ux = t // 9, t % 9 // 3, t % 3
        w = []
        for uz in range(3):
            k = uy * 9 + uz * 3 + ux
            k = k + f * (53 - 2 * k)
            block = wt[pl.ds(pl.multiple_of(k * 8, 8), 8), :]
            w.append(jnp.concatenate([block, block], axis=0))
        at = [band_block(w, -2 * i) for i in range(4)]
        before, after = band_block(w, -8), band_block(w, 2)
        zero = jnp.zeros((16, 128), BF)
        for pair in range(16):
            own = pair // 4
            cells = [zero] * 4
            cells[own] = at[pair % 4]
            if pair % 4 == 0 and own > 0:
                cells[own - 1] = before
            if pair % 4 == 3 and own < 3:
                cells[own + 1] = after
            rows_at = pl.multiple_of(t * 256 + pair * 16, 16)
            band[pl.ds(rows_at, 16), :] = jnp.concatenate(cells, axis=1)
        return carry

    lax.fori_loop(0, 18, build, 0)

    def turn(t, carry):
        rows_at = pl.multiple_of(t * 256, 256)
        turned_at = pl.multiple_of(t // 3 * 512, 512)
        turned_band[t % 3, pl.ds(turned_at, 512), :] = band[pl.ds(rows_at, 256), :].T
        return carry

    lax.fori_loop(0, 9, turn, 0)

    def halo_copies(f):
        return (remote(planes.at[f, 1], planes.at[f, 0], semh, f, right),
                remote(planes.at[f, 1], planes.at[f, 2], semh, 2 + f, left))

    for f in range(2):
        wait_all(*ex1[f])
        parts = [jnp.concatenate([r1[f, k], r1[f, 8 + k]], axis=0).astype(F32) for k in range(8)]
        whole = jnp.concatenate(swap_blocks(parts), axis=0).astype(BF)
        s2[f] = mm(pbt[...], whole).astype(BF).reshape(16, 16, 256)
        send_all(*ex2[f])
        r2[f, b] = s2[f, b]

    loads[3].wait()
    loads[4].wait()
    for f in range(2):
        wait_sent(*ex1[f])
    for f in range(2):
        wait_all(*ex2[f])
        v = to_volume(r2[f].reshape(256, 256), (wy[...], wy_low[...]), (mz[...], mz_low[...]))
        planes[f, 1] = (v if f == 0 else -v).astype(BF)
        for c in halo_copies(f):
            c.start()

    for f in range(2):
        wait_sent(*ex2[f])
    convolved = []
    for f in range(2):
        for c in halo_copies(f):
            c.wait()

        @pl.when(x == 0)
        def _():
            planes[f, 0] = jnp.zeros((256, 256), BF)

        @pl.when(x == 255)
        def _():
            planes[f, 2] = jnp.zeros((256, 256), BF)

        cat = jnp.concatenate([planes[f, ux] for ux in range(3)], axis=1)
        total = None
        for uy in (-1, 0, 1):
            row = f * 2304 + (uy + 1) * 768
            v = shifted(mm(cat, band[row:row + 768, :]), uy)
            total = v if total is None else total + v
        convolved.append(total)

    active, back_hidden = gates(*convolved)
    for uy in (-1, 0, 1):
        bh[:, (uy + 1) * 512:(uy + 2) * 512] = shifted(back_hidden, -uy).astype(BF)

    def share(side):
        return mm(bh[...], turned_band[side])

    away = x % 2
    near = 1 - away
    share_copies = []
    for i, side in enumerate((away, near)):
        send_p[i] = share(2 * side).astype(BF)
        c = remote(send_p.at[i], recv_p.at[i], semp, i, at_x((x + 255 + 2 * side) % 256))
        c.start()
        share_copies.append(c)
    own = share(1)

    lane = lax.broadcasted_iota(jnp.int32, (512, 256), 1)
    for f, v in enumerate((back_hidden, active)):
        v = v.T
        zt[f, 0] = jnp.where(lane == 255, 0.0, roll(v, 255, 1)).astype(BF)
        zt[f, 1] = v.astype(BF)
        zt[f, 2] = jnp.where(lane == 0, 0.0, roll(v, 1, 1)).astype(BF)
    for t in range(18):
        gm = mm(zt[t // 9, t % 9 // 3], planes[t // 9, t % 3])
        for u, v in enumerate(band_sums(gm)):
            k = t * 3 + u
            g_lanes[k * 16:(k + 1) * 16, :] = v
    sums = lane_sums(g_lanes[...])
    slot = lax.broadcasted_iota(jnp.int32, (16, 128), 1) // 8
    for tile in range(8):
        v = jnp.zeros((16, 128), F32)
        for at in range(7):
            k = 7 * tile + at
            if k < 54:
                v = jnp.where(slot == at, sums[k * 16:(k + 1) * 16], v)
        gr[2 * tile] = v[:8]
        gr[2 * tile + 1] = v[8:]
    exg1 = (m, dev1, lambda p: gr.at[p], lambda p: ga.at[p], (gr.at[0:15], ga.at[0:15]), semg1)
    send_all(*exg1)
    ga[m] = gr[m]

    for c in share_copies:
        c.wait()
    inside = jnp.where((x > 0) & (x < 255), 1.0, 0.0)
    back_image = own + recv_p[0].astype(F32) * inside + recv_p[1].astype(F32)

    s3[...] = from_volume(back_image, wyt[...], mzt[...]).reshape(16, 16, 256)
    ex3 = (b, dev2, lambda p: s3.at[p], lambda p: r3.at[p], (s3.at[0:15], r3.at[0:15]), sem3)
    send_all(*ex3)
    r3[b] = s3[b]

    wait_all(*exg1)
    gs[...] = jnp.broadcast_to(jnp.sum(ga[...], axis=0, keepdims=True), (16, 8, 128))
    exg2 = (b, dev2, lambda p: gs.at[p], lambda p: gb.at[p], (gs.at[0:15], gb.at[0:15]), semg2)
    send_all(*exg2)
    gb[b] = gs[b]

    wait_all(*ex3)
    rows = mm(pb[...], r3[...].reshape(256, 256))
    parts = swap_blocks([rows[k * 32:(k + 1) * 32] for k in range(8)])
    for k in range(8):
        v = parts[k].astype(BF)
        s4[k] = v[:16]
        s4[8 + k] = v[16:]
    ex4 = (m, dev1, lambda p: s4.at[p], lambda p: r4.at[p], (s4.at[0:15], r4.at[0:15]), sem4)
    send_all(*ex4)
    r4[m] = s4[m]

    wait_all(*exg2)
    gt[...] = jnp.broadcast_to(jnp.sum(gb[...], axis=0, keepdims=True), (16, 8, 128))
    exg3 = (m, dev1, lambda p: gt.at[p], lambda p: gc.at[p], (gt.at[0:15], gc.at[0:15]), semg3)
    send_all(*exg3)
    gc[m] = gt[m]

    for e in (ex3, ex4, exg1, exg2, exg3):
        wait_sent(*e)
    wait_all(*ex4)
    spectrum = unpack(r4[...].reshape(256, 256), qyt[...], pxt[...])
    factor = mask[...].astype(F32)
    eye = lax.broadcasted_iota(jnp.int32, (8, 8), 0) == lax.broadcasted_iota(jnp.int32, (8, 8), 1)
    for z in range(4):
        rows = cotangent[:, z, :]
        sampled = jnp.sum(jnp.where(eye, factor[z:z + 1], 0.0), axis=1, keepdims=True) * consistency[0]
        scaled = (rows.reshape(8, 8, 256) * sampled[None]).reshape(64, 256)
        out[:, z, :] = rows - scaled + spectrum[z * 64:(z + 1) * 64]

    wait_all(*exg3)
    turned = gc[...].reshape(128, 128).T
    for t in range(8):
        at_front = turned if t == 0 else roll(turned, 128 - 16 * t, 1)
        for slot_at in range(7):
            k = 7 * t + slot_at
            if k < 54:
                f, uy, ux, uz = k // 27, k // 9 % 3, k // 3 % 3, k % 3
                n = uy * 9 + uz * 3 + ux
                block = at_front[slot_at * 8:slot_at * 8 + 8, :16]
                if f == 0:
                    grad_in[n] = block
                else:
                    grad_out[26 - n] = block


def local(kspace, cotangent, weight_in, weight_out, consistency_weight, sampling_mask):
    w_in = weight_in.transpose(2, 3, 4, 1, 0).reshape(27, 8, 16)
    w_out = weight_out.transpose(2, 3, 4, 0, 1).reshape(27, 8, 16)
    vmem = pl.BlockSpec(memory_space=pltpu.VMEM)
    hbm = pl.BlockSpec(memory_space=pltpu.HBM)

    def scratch(*shape, kind=BF):
        return pltpu.VMEM(shape, kind)

    def sems(n):
        return pltpu.SemaphoreType.DMA((2, n))

    grad_shape = jax.ShapeDtypeStruct((27, 8, 16), F32)
    out, grad_in, grad_out = pl.pallas_call(
        kernel,
        out_shape=(pltpu.VMEM((64, 4, 256), F32), pltpu.VMEM((27, 8, 16), F32), pltpu.VMEM((27, 8, 16), F32)),
        in_specs=[hbm, hbm, vmem, vmem, vmem, pl.BlockSpec(memory_space=pltpu.SMEM), hbm, hbm, hbm],
        out_specs=(vmem, vmem, vmem),
        scratch_shapes=[
            scratch(64, 4, 256, kind=F32), scratch(64, 4, 256, kind=F32),
            scratch(768, 256), scratch(512, 512), scratch(2816, 256), scratch(432, 128, kind=F32),
            pltpu.SemaphoreType.DMA((5,)),
            scratch(2, 16, 16, 256), scratch(2, 16, 16, 256), scratch(2, 16, 16, 256), scratch(2, 16, 16, 256),
            scratch(2, 3, 256, 256), scratch(4608, 512), scratch(3, 1536, 256), scratch(2, 3, 512, 256), scratch(256, 1536),
            scratch(2, 256, 256), scratch(2, 256, 256),
            scratch(16, 16, 256), scratch(16, 16, 256),
            scratch(16, 16, 256), scratch(16, 16, 256),
            scratch(864, 128, kind=F32), *[scratch(16, 8, 128, kind=F32) for _ in range(6)],
            pltpu.SemaphoreType.DMA((2, 2, 1)), pltpu.SemaphoreType.DMA((2, 2, 1)), sems(4), sems(2), sems(1), sems(1), sems(1), sems(1), sems(1),
        ],
        compiler_params=pltpu.CompilerParams(
            collective_id=0, has_side_effects=True, vmem_limit_bytes=60 * 1024 * 1024),
        name="cascade",
    )(kspace.reshape(64, 4, 256), cotangent.reshape(64, 4, 256), sampling_mask.T, w_in, w_out, consistency_weight, *map(jnp.asarray, tables()))
    scale = 1.0 / math.sqrt(2097152)
    grad_in = (grad_in * scale).reshape(3, 3, 3, 8, 16).transpose(4, 3, 0, 1, 2)
    grad_out = (grad_out * scale).reshape(3, 3, 3, 8, 16).transpose(3, 4, 0, 1, 2)
    return out.reshape(kspace.shape), grad_in, grad_out


def solution(mesh):
    placed = P(None, None, "gy", "gz", None)
    return jax.shard_map(
        local,
        mesh=mesh,
        in_specs=(placed, placed, P(), P(), P(), P("gy", "gz")),
        out_specs=(placed, P(), P()),
        check_vma=False,
    )
```

```python
import math

import jax
import jax.numpy as jnp
import numpy as np
from jax import lax
from jax.experimental import pallas as pl
from jax.experimental.pallas import tpu as pltpu
from jax.sharding import PartitionSpec as P

BF = jnp.bfloat16
F32 = jnp.float32
NT = (((1,), (1,)), ((), ()))
roll = pltpu.roll


def mm(a, b):
    return jnp.dot(a, b, preferred_element_type=F32)


def mm_nt(a, b):
    return lax.dot_general(a, b, NT, preferred_element_type=F32)


def plane_of(m, b):
    return b * 16 + m


def member_of(x):
    return x % 16, x // 16


def tables():
    z_l, pc, y_l = np.meshgrid(np.arange(4), np.arange(8), np.arange(8), indexing="ij")
    qy = np.zeros((256, 256), np.float32)
    qy[(y_l * 32 + z_l * 8 + pc).ravel(), (z_l * 64 + pc * 8 + y_l).ravel()] = 1
    m, b = np.meshgrid(np.arange(16), np.arange(16), indexing="ij")
    px = np.zeros((256, 256), np.float32)
    px[(m * 16 + b).ravel(), plane_of(m, b).ravel()] = 1
    b, h, y = np.meshgrid(np.arange(16), np.arange(2), np.arange(8), indexing="ij")
    pb = np.zeros((256, 256), np.float32)
    pb[(y * 32 + h * 16 + b).ravel(), (b * 16 + h * 8 + y).ravel()] = 1
    ky = (128 * h + 8 * b + y).ravel()
    theta = 2 * np.pi * ((np.arange(256)[:, None] * ky[None, :]) % 256) / 256
    wy = np.concatenate([np.cos(theta), np.sin(theta)], 0) / 16
    j, z_l, c = np.meshgrid(np.arange(8), np.arange(4), np.arange(4), indexing="ij")
    kz = (4 * j + z_l).ravel()
    row = (j * 32 + z_l * 8 + c).ravel()
    col = c.ravel()
    mz = np.zeros((512, 256), np.float64)
    for z in range(32):
        phi = 2 * np.pi * ((kz * z) % 32) / 32
        cs, sn = np.cos(phi) / math.sqrt(32), np.sin(phi) / math.sqrt(32)
        re, im = z * 8 + col, z * 8 + 4 + col
        mz[row, re] = cs
        mz[row + 4, re] = -sn
        mz[row, im] = sn
        mz[row + 4, im] = cs
        mz[256 + row, re] = -sn
        mz[256 + row + 4, re] = -cs
        mz[256 + row, im] = cs
        mz[256 + row + 4, im] = -sn
    out = {"qy": qy, "px": px, "pbt": pb.T, "pb": pb, "wy": wy, "mz": mz, "qyt": qy.T, "pxt": px.T}
    out["wyt"] = np.concatenate([wy[:256].T, wy[256:].T], 1)
    out["mzt"] = np.concatenate([mz[:256].T, mz[256:].T], 1)
    high = {k: v.astype(np.float32).astype(BF) for k, v in out.items()}
    low = {k: (out[k] - high[k].astype(np.float64)).astype(np.float32).astype(BF) for k in ("wy", "mz")}
    first = np.concatenate([high["qy"], high["px"], high["pbt"]])
    wide = np.concatenate([high["wyt"], high["mzt"]])
    rest = np.concatenate([high["wy"], low["wy"], high["mz"], low["mz"], high["pb"], high["qyt"], high["pxt"]])
    return first, wide, rest


def pack(x, qy, px):
    u = mm(qy, x.astype(BF)).astype(BF)
    return mm_nt(px, u).astype(BF)


def unpack(a, qyt, pxt):
    u = mm(pxt, a).astype(BF)
    return mm_nt(qyt, u)


def swap_four(parts):
    parts = list(parts)
    block = lax.broadcasted_iota(jnp.int32, parts[0].shape, 1) // 32
    for bit in (1, 2):
        low = (block & bit) == 0
        for j in range(4):
            if not j & bit:
                a, b = parts[j], parts[j | bit]
                parts[j] = jnp.where(low, a, roll(b, 32 * bit, 1))
                parts[j | bit] = jnp.where(low, roll(a, 128 - 32 * bit, 1), b)
    return parts


def swap_blocks(parts):
    out = []
    for y in (0, 128):
        low, high = (swap_four([p[:, y:y + 128] for p in parts[k:k + 4]]) for k in (0, 4))
        out += [jnp.concatenate([a, c], axis=1) for a, c in zip(low, high)]
    return out


def to_volume(d, wy, mz):
    cs = mm(jnp.concatenate(wy, axis=1), jnp.concatenate([d, d], axis=0))
    cs = jnp.concatenate([cs[:256], cs[256:]], axis=1)
    high = cs.astype(BF)
    low = (cs - high.astype(F32)).astype(BF)
    return mm(jnp.concatenate([high, high, low], axis=1), jnp.concatenate([mz[0], mz[1], mz[0]], axis=0))


def from_volume(v, wyt, mzt):
    e = mm(v.astype(BF), mzt).astype(BF)
    half = e.shape[1] // 2
    return mm(wyt, jnp.concatenate([e[:, :half], e[:, half:]], axis=0)).astype(BF)


def shifted(v, u):
    if u == 0:
        return v
    row = lax.broadcasted_iota(jnp.int32, v.shape, 0)
    n = v.shape[0]
    if u == 1:
        return jnp.where(row == n - 1, 0.0, roll(v, n - 1, 0))
    return jnp.where(row == 0, 0.0, roll(v, 1, 0))


def band_block(w, start):
    lane = lax.broadcasted_iota(jnp.int32, (16, 128), 1)
    row = lax.broadcasted_iota(jnp.int32, (16, 128), 0)
    u = row // 8 - start - lane // 16
    return jnp.where(u == -1, w[0], jnp.where(u == 0, w[1], jnp.where(u == 1, w[2], 0.0))).astype(BF)


def band_sums(g):
    cell = lax.broadcasted_iota(jnp.int32, (16, 128), 1) // 8
    kept = [[jnp.zeros((16, 128), F32) for _ in range(3)] for _ in range(2)]
    for z in range(32):
        for half in range(2):
            if 16 * half - 1 <= z <= 16 * half + 16:
                t = cell + (16 * half - z)
                kept[half][z % 3] = jnp.where(t * t <= 1, g[z * 16:(z + 1) * 16, 128 * half:128 * (half + 1)], kept[half][z % 3])
    out = []
    for u in (-1, 0, 1):
        total = None
        for half in range(2):
            z = cell + (16 * half - u)
            r = (z + 3) % 3
            s = jnp.where(r == 0, kept[half][0], jnp.where(r == 1, kept[half][1], kept[half][2]))
            s = jnp.where((z >= 0) & (z < 32), s, 0.0)
            total = s if total is None else total + s
        out.append(total)
    return out


def lane_sums(v):
    same = (lax.broadcasted_iota(jnp.int32, (128, 128), 0) % 8 == lax.broadcasted_iota(jnp.int32, (128, 128), 1) % 8).astype(BF)
    total = None
    for _ in range(3):
        part = v.astype(BF)
        v = v - part.astype(F32)
        term = mm(part, same)
        total = term if total is None else total + term
    return total


def gates(hidden, back_active):
    gate = jax.nn.sigmoid(hidden)
    return hidden * gate, back_active * gate * (1.0 + hidden * (1.0 - gate))


def kernel(kspace_hbm, cotangent_hbm, mask, weight_in, weight_out, consistency, first_hbm, wide_hbm, rest_hbm,
           out, grad_in, grad_out,
           kspace, cotangent, first, wide, rest, wt, seml,
           a1, r1, s2, r2, planes, band, turned_band, zt, bh, send_p, recv_p, s3, r3, s4, r4, g_lanes, gr, ga, gs, gb, gt, gc,
           sem1, sem2, semh, semp, sem3, sem4, semg1, semg2, semg3):
    g = lax.axis_index("gy")
    j = lax.axis_index("gz")
    h, b = g // 16, g % 16
    m = h * 8 + j

    def dev1(p):
        return (lax.div(p, 8) * 16 + b, lax.rem(p, 8))

    def dev2(p):
        return (h * 16 + p, j)

    def at_x(p):
        member, place = member_of(p)
        return ((member // 8) * 16 + place, member % 8)

    x = plane_of(m, b)
    right = at_x((x + 1) % 256)
    left = at_x((x + 255) % 256)

    loads = [pltpu.make_async_copy(src, dst, seml.at[i]) for i, (src, dst) in enumerate((
        (first_hbm, first), (kspace_hbm, kspace), (cotangent_hbm, cotangent), (rest_hbm, rest), (wide_hbm, wide)))]
    for c in loads:
        c.start()
    barrier = pltpu.get_barrier_semaphore()

    for d in range(1, 16):
        pl.semaphore_signal(barrier, inc=1, device_id=dev1(lax.rem(m + d, 16)), device_id_type=pl.DeviceIdType.MESH)
        pl.semaphore_signal(barrier, inc=1, device_id=dev2(lax.rem(b + d, 16)), device_id_type=pl.DeviceIdType.MESH)
    pl.semaphore_signal(barrier, inc=1, device_id=right, device_id_type=pl.DeviceIdType.MESH)
    pl.semaphore_signal(barrier, inc=1, device_id=left, device_id_type=pl.DeviceIdType.MESH)

    qy, px, pbt = (first.at[256 * i:256 * (i + 1)] for i in range(3))
    wyt, mzt = (wide.at[256 * i:256 * (i + 1)] for i in range(2))
    wy, wy_low, mz, mz_low = (rest.at[512 * i:512 * (i + 1)] for i in range(4))
    pb, qyt, pxt = (rest.at[2048 + 256 * i:2304 + 256 * i] for i in range(3))

    def remote(src, dst, sems, i, device):
        return pltpu.make_async_remote_copy(
            src_ref=src, dst_ref=dst, send_sem=sems.at[0, i], recv_sem=sems.at[1, i],
            device_id=device, device_id_type=pl.DeviceIdType.MESH)

    def send_all(me, dev, src, dst, some, sems):
        for d in (8, 7, 9, 6, 10, 5, 11, 4, 12, 3, 13, 2, 14, 1, 15):
            p = lax.rem(me + d, 16)
            remote(src(p), dst(me), sems, 0, dev(p)).start()

    def wait_all(me, dev, src, dst, some, sems):
        remote(*some, sems, 0, dev(lax.rem(me + 1, 16))).wait_recv()

    def wait_sent(me, dev, src, dst, some, sems):
        remote(*some, sems, 0, dev(lax.rem(me + 1, 16))).wait_send()

    ex1 = [(m, dev1, lambda p, f=f: a1.at[f, p], lambda p, f=f: r1.at[f, p],
            (a1.at[f, 0:15], r1.at[f, 0:15]), sem1.at[f]) for f in range(2)]
    ex2 = [(b, dev2, lambda p, f=f: s2.at[f, p], lambda p, f=f: r2.at[f, p],
            (s2.at[f, 0:15], r2.at[f, 0:15]), sem2.at[f]) for f in range(2)]
    loads[0].wait()
    for f, field in enumerate((kspace, cotangent)):
        loads[1 + f].wait()
        rows = jnp.concatenate([field[:, z, :] for z in range(4)], axis=0)
        a1[f] = pack(rows, qy[...], px[...]).reshape(16, 16, 256)
        if f == 0:
            pl.semaphore_wait(barrier, 32)
        send_all(*ex1[f])
        r1[f, m] = a1[f, m]

    spread = (lax.broadcasted_iota(jnp.int32, (16, 128), 1) % 16 == lax.broadcasted_iota(jnp.int32, (16, 128), 0)).astype(BF)
    for f, w in enumerate((weight_in, weight_out)):
        wt[216 * f:216 * (f + 1), :] = mm(w[...].astype(F32).reshape(216, 16).astype(BF), spread)

    def build(t, carry):
        f, uy, ux = t // 9, t % 9 // 3, t % 3
        w = []
        for uz in range(3):
            k = uy * 9 + uz * 3 + ux
            k = k + f * (53 - 2 * k)
            block = wt[pl.ds(pl.multiple_of(k * 8, 8), 8), :]
            w.append(jnp.concatenate([block, block], axis=0))
        at = [band_block(w, -2 * i) for i in range(4)]
        before, after = band_block(w, -8), band_block(w, 2)
        zero = jnp.zeros((16, 128), BF)
        for pair in range(16):
            own = pair // 4
            cells = [zero] * 4
            cells[own] = at[pair % 4]
            if pair % 4 == 0 and own > 0:
                cells[own - 1] = before
            if pair % 4 == 3 and own < 3:
                cells[own + 1] = after
            rows_at = pl.multiple_of(t * 256 + pair * 16, 16)
            band[pl.ds(rows_at, 16), :] = jnp.concatenate(cells, axis=1)
        return carry

    lax.fori_loop(0, 18, build, 0)

    def turn(t, carry):
        rows_at = pl.multiple_of(t * 256, 256)
        turned_at = pl.multiple_of(t // 3 * 512, 512)
        turned_band[t % 3, pl.ds(turned_at, 512), :] = band[pl.ds(rows_at, 256), :].T
        return carry

    lax.fori_loop(0, 9, turn, 0)

    def halo_copies(f):
        return (remote(planes.at[f, 1], planes.at[f, 0], semh, f, right),
                remote(planes.at[f, 1], planes.at[f, 2], semh, 2 + f, left))

    for f in range(2):
        wait_all(*ex1[f])
        parts = [jnp.concatenate([r1[f, k], r1[f, 8 + k]], axis=0).astype(F32) for k in range(8)]
        whole = jnp.concatenate(swap_blocks(parts), axis=0).astype(BF)
        s2[f] = mm(pbt[...], whole).astype(BF).reshape(16, 16, 256)
        send_all(*ex2[f])
        r2[f, b] = s2[f, b]

    loads[3].wait()
    loads[4].wait()
    for f in range(2):
        wait_sent(*ex1[f])
    for f in range(2):
        wait_all(*ex2[f])
        v = to_volume(r2[f].reshape(256, 256), (wy[...], wy_low[...]), (mz[...], mz_low[...]))
        planes[f, 1] = (v if f == 0 else -v).astype(BF)
        for c in halo_copies(f):
            c.start()

    for f in range(2):
        wait_sent(*ex2[f])
    convolved = []
    for f in range(2):
        for c in halo_copies(f):
            c.wait()

        @pl.when(x == 0)
        def _():
            planes[f, 0] = jnp.zeros((256, 256), BF)

        @pl.when(x == 255)
        def _():
            planes[f, 2] = jnp.zeros((256, 256), BF)

        cat = jnp.concatenate([planes[f, ux] for ux in range(3)], axis=1)
        total = None
        for uy in (-1, 0, 1):
            row = f * 2304 + (uy + 1) * 768
            v = shifted(mm(cat, band[row:row + 768, :]), uy)
            total = v if total is None else total + v
        convolved.append(total)

    active, back_hidden = gates(*convolved)
    for uy in (-1, 0, 1):
        bh[:, (uy + 1) * 512:(uy + 2) * 512] = shifted(back_hidden, -uy).astype(BF)

    def share(side):
        return mm(bh[...], turned_band[side])

    away = x % 2
    near = 1 - away
    share_copies = []
    for i, side in enumerate((away, near)):
        send_p[i] = share(2 * side).astype(BF)
        c = remote(send_p.at[i], recv_p.at[i], semp, i, at_x((x + 255 + 2 * side) % 256))
        c.start()
        share_copies.append(c)
    own = share(1)

    lane = lax.broadcasted_iota(jnp.int32, (512, 256), 1)
    for f, v in enumerate((back_hidden, active)):
        v = v.T
        zt[f, 0] = jnp.where(lane == 255, 0.0, roll(v, 255, 1)).astype(BF)
        zt[f, 1] = v.astype(BF)
        zt[f, 2] = jnp.where(lane == 0, 0.0, roll(v, 1, 1)).astype(BF)
    for t in range(18):
        gm = mm(zt[t // 9, t % 9 // 3], planes[t // 9, t % 3])
        for u, v in enumerate(band_sums(gm)):
            k = t * 3 + u
            g_lanes[k * 16:(k + 1) * 16, :] = v
    sums = lane_sums(g_lanes[...])
    slot = lax.broadcasted_iota(jnp.int32, (16, 128), 1) // 8
    for tile in range(8):
        v = jnp.zeros((16, 128), F32)
        for at in range(7):
            k = 7 * tile + at
            if k < 54:
                v = jnp.where(slot == at, sums[k * 16:(k + 1) * 16], v)
        gr[2 * tile] = v[:8]
        gr[2 * tile + 1] = v[8:]
    exg1 = (m, dev1, lambda p: gr.at[p], lambda p: ga.at[p], (gr.at[0:15], ga.at[0:15]), semg1)
    send_all(*exg1)
    ga[m] = gr[m]

    for c in share_copies:
        c.wait()
    inside = jnp.where((x > 0) & (x < 255), 1.0, 0.0)
    back_image = own + recv_p[0].astype(F32) * inside + recv_p[1].astype(F32)

    s3[...] = from_volume(back_image, wyt[...], mzt[...]).reshape(16, 16, 256)
    ex3 = (b, dev2, lambda p: s3.at[p], lambda p: r3.at[p], (s3.at[0:15], r3.at[0:15]), sem3)
    send_all(*ex3)
    r3[b] = s3[b]

    wait_all(*exg1)
    gs[...] = jnp.broadcast_to(jnp.sum(ga[...], axis=0, keepdims=True), (16, 8, 128))
    exg2 = (b, dev2, lambda p: gs.at[p], lambda p: gb.at[p], (gs.at[0:15], gb.at[0:15]), semg2)
    send_all(*exg2)
    gb[b] = gs[b]

    wait_all(*ex3)
    rows = mm(pb[...], r3[...].reshape(256, 256))
    parts = swap_blocks([rows[k * 32:(k + 1) * 32] for k in range(8)])
    for k in range(8):
        v = parts[k].astype(BF)
        s4[k] = v[:16]
        s4[8 + k] = v[16:]
    ex4 = (m, dev1, lambda p: s4.at[p], lambda p: r4.at[p], (s4.at[0:15], r4.at[0:15]), sem4)
    send_all(*ex4)
    r4[m] = s4[m]

    wait_all(*exg2)
    gt[...] = jnp.broadcast_to(jnp.sum(gb[...], axis=0, keepdims=True), (16, 8, 128))
    exg3 = (m, dev1, lambda p: gt.at[p], lambda p: gc.at[p], (gt.at[0:15], gc.at[0:15]), semg3)
    send_all(*exg3)
    gc[m] = gt[m]

    for e in (ex3, ex4, exg1, exg2, exg3):
        wait_sent(*e)
    wait_all(*ex4)
    spectrum = unpack(r4[...].reshape(256, 256), qyt[...], pxt[...])
    factor = mask[...].astype(F32)
    eye = lax.broadcasted_iota(jnp.int32, (8, 8), 0) == lax.broadcasted_iota(jnp.int32, (8, 8), 1)
    for z in range(4):
        rows = cotangent[:, z, :]
        sampled = jnp.sum(jnp.where(eye, factor[z:z + 1], 0.0), axis=1, keepdims=True) * consistency[0]
        scaled = (rows.reshape(8, 8, 256) * sampled[None]).reshape(64, 256)
        out[:, z, :] = rows - scaled + spectrum[z * 64:(z + 1) * 64]

    wait_all(*exg3)
    turned = gc[...].reshape(128, 128).T
    for t in range(8):
        at_front = turned if t == 0 else roll(turned, 128 - 16 * t, 1)
        for slot_at in range(7):
            k = 7 * t + slot_at
            if k < 54:
                f, uy, ux, uz = k // 27, k // 9 % 3, k // 3 % 3, k % 3
                n = uy * 9 + uz * 3 + ux
                block = at_front[slot_at * 8:slot_at * 8 + 8, :16]
                if f == 0:
                    grad_in[n] = block
                else:
                    grad_out[26 - n] = block


def local(kspace, cotangent, weight_in, weight_out, consistency_weight, sampling_mask):
    w_in = weight_in.transpose(2, 3, 4, 1, 0).reshape(27, 8, 16)
    w_out = weight_out.transpose(2, 3, 4, 0, 1).reshape(27, 8, 16)
    vmem = pl.BlockSpec(memory_space=pltpu.VMEM)
    hbm = pl.BlockSpec(memory_space=pltpu.HBM)

    def scratch(*shape, kind=BF):
        return pltpu.VMEM(shape, kind)

    def sems(n):
        return pltpu.SemaphoreType.DMA((2, n))

    grad_shape = jax.ShapeDtypeStruct((27, 8, 16), F32)
    out, grad_in, grad_out = pl.pallas_call(
        kernel,
        out_shape=(pltpu.VMEM((64, 4, 256), F32), pltpu.VMEM((27, 8, 16), F32), pltpu.VMEM((27, 8, 16), F32)),
        in_specs=[hbm, hbm, vmem, vmem, vmem, pl.BlockSpec(memory_space=pltpu.SMEM), hbm, hbm, hbm],
        out_specs=(vmem, vmem, vmem),
        scratch_shapes=[
            scratch(64, 4, 256, kind=F32), scratch(64, 4, 256, kind=F32),
            scratch(768, 256), scratch(512, 512), scratch(2816, 256), scratch(432, 128, kind=F32),
            pltpu.SemaphoreType.DMA((5,)),
            scratch(2, 16, 16, 256), scratch(2, 16, 16, 256), scratch(2, 16, 16, 256), scratch(2, 16, 16, 256),
            scratch(2, 3, 256, 256), scratch(4608, 512), scratch(3, 1536, 256), scratch(2, 3, 512, 256), scratch(256, 1536),
            scratch(2, 256, 256), scratch(2, 256, 256),
            scratch(16, 16, 256), scratch(16, 16, 256),
            scratch(16, 16, 256), scratch(16, 16, 256),
            scratch(864, 128, kind=F32), *[scratch(16, 8, 128, kind=F32) for _ in range(6)],
            pltpu.SemaphoreType.DMA((2, 2, 1)), pltpu.SemaphoreType.DMA((2, 2, 1)), sems(4), sems(2), sems(1), sems(1), sems(1), sems(1), sems(1),
        ],
        compiler_params=pltpu.CompilerParams(
            collective_id=0, has_side_effects=True, vmem_limit_bytes=60 * 1024 * 1024),
        name="cascade",
    )(kspace.reshape(64, 4, 256), cotangent.reshape(64, 4, 256), sampling_mask.T, w_in, w_out, consistency_weight, *map(jnp.asarray, tables()))
    scale = 1.0 / math.sqrt(2097152)
    grad_in = (grad_in * scale).reshape(3, 3, 3, 8, 16).transpose(4, 3, 0, 1, 2)
    grad_out = (grad_out * scale).reshape(3, 3, 3, 8, 16).transpose(3, 4, 0, 1, 2)
    return out.reshape(kspace.shape), grad_in, grad_out


def solution(mesh):
    placed = P(None, None, "gy", "gz", None)
    return jax.shard_map(
        local,
        mesh=mesh,
        in_specs=(placed, placed, P(), P(), P(), P("gy", "gz")),
        out_specs=(placed, P(), P()),
        check_vma=False,
    )
```

```python
import math

import jax
import jax.numpy as jnp
import numpy as np
from jax import lax
from jax.experimental import pallas as pl
from jax.experimental.pallas import tpu as pltpu
from jax.sharding import PartitionSpec as P

BF = jnp.bfloat16
F32 = jnp.float32
NT = (((1,), (1,)), ((), ()))
roll = pltpu.roll


def mm(a, b):
    return jnp.dot(a, b, preferred_element_type=F32)


def mm_nt(a, b):
    return lax.dot_general(a, b, NT, preferred_element_type=F32)


def plane_of(m, b):
    return b * 16 + m


def member_of(x):
    return x % 16, x // 16


def tables():
    z_l, pc, y_l = np.meshgrid(np.arange(4), np.arange(8), np.arange(8), indexing="ij")
    qy = np.zeros((256, 256), np.float32)
    qy[(y_l * 32 + z_l * 8 + pc).ravel(), (z_l * 64 + pc * 8 + y_l).ravel()] = 1
    m, b = np.meshgrid(np.arange(16), np.arange(16), indexing="ij")
    px = np.zeros((256, 256), np.float32)
    px[(m * 16 + b).ravel(), plane_of(m, b).ravel()] = 1
    b, h, y = np.meshgrid(np.arange(16), np.arange(2), np.arange(8), indexing="ij")
    pb = np.zeros((256, 256), np.float32)
    pb[(y * 32 + h * 16 + b).ravel(), (b * 16 + h * 8 + y).ravel()] = 1
    ky = (128 * h + 8 * b + y).ravel()
    theta = 2 * np.pi * ((np.arange(256)[:, None] * ky[None, :]) % 256) / 256
    wy = np.concatenate([np.cos(theta), np.sin(theta)], 0) / 16
    j, z_l, c = np.meshgrid(np.arange(8), np.arange(4), np.arange(4), indexing="ij")
    kz = (4 * j + z_l).ravel()
    row = (j * 32 + z_l * 8 + c).ravel()
    col = c.ravel()
    mz = np.zeros((512, 256), np.float64)
    for z in range(32):
        phi = 2 * np.pi * ((kz * z) % 32) / 32
        cs, sn = np.cos(phi) / math.sqrt(32), np.sin(phi) / math.sqrt(32)
        re, im = z * 8 + col, z * 8 + 4 + col
        mz[row, re] = cs
        mz[row + 4, re] = -sn
        mz[row, im] = sn
        mz[row + 4, im] = cs
        mz[256 + row, re] = -sn
        mz[256 + row + 4, re] = -cs
        mz[256 + row, im] = cs
        mz[256 + row + 4, im] = -sn
    out = {"qy": qy, "px": px, "pbt": pb.T, "pb": pb, "wy": wy, "mz": mz, "qyt": qy.T, "pxt": px.T}
    out["wyt"] = np.concatenate([wy[:256].T, wy[256:].T], 1)
    out["mzt"] = np.concatenate([mz[:256].T, mz[256:].T], 1)
    high = {k: v.astype(np.float32).astype(BF) for k, v in out.items()}
    low = {k: (out[k] - high[k].astype(np.float64)).astype(np.float32).astype(BF) for k in ("wy", "mz")}
    first = np.concatenate([high["qy"], high["px"], high["pbt"]])
    wide = np.concatenate([high["wyt"], high["mzt"]])
    rest = np.concatenate([high["wy"], low["wy"], high["mz"], low["mz"], high["pb"], high["qyt"], high["pxt"]])
    return first, wide, rest


def pack(x, qy, px):
    u = mm(qy, x.astype(BF)).astype(BF)
    return mm_nt(px, u).astype(BF)


def unpack(a, qyt, pxt):
    u = mm(pxt, a).astype(BF)
    return mm_nt(qyt, u)


def swap_four(parts):
    parts = list(parts)
    block = lax.broadcasted_iota(jnp.int32, parts[0].shape, 1) // 32
    for bit in (1, 2):
        low = (block & bit) == 0
        for j in range(4):
            if not j & bit:
                a, b = parts[j], parts[j | bit]
                parts[j] = jnp.where(low, a, roll(b, 32 * bit, 1))
                parts[j | bit] = jnp.where(low, roll(a, 128 - 32 * bit, 1), b)
    return parts


def swap_blocks(parts):
    out = []
    for y in (0, 128):
        low, high = (swap_four([p[:, y:y + 128] for p in parts[k:k + 4]]) for k in (0, 4))
        out += [jnp.concatenate([a, c], axis=1) for a, c in zip(low, high)]
    return out


def to_volume(d, wy, mz):
    cs = mm(jnp.concatenate(wy, axis=1), jnp.concatenate([d, d], axis=0))
    cs = jnp.concatenate([cs[:256], cs[256:]], axis=1)
    high = cs.astype(BF)
    low = (cs - high.astype(F32)).astype(BF)
    return mm(jnp.concatenate([high, high, low], axis=1), jnp.concatenate([mz[0], mz[1], mz[0]], axis=0))


def from_volume(v, wyt, mzt):
    e = mm(v.astype(BF), mzt).astype(BF)
    half = e.shape[1] // 2
    return mm(wyt, jnp.concatenate([e[:, :half], e[:, half:]], axis=0)).astype(BF)


def shifted(v, u):
    if u == 0:
        return v
    row = lax.broadcasted_iota(jnp.int32, v.shape, 0)
    n = v.shape[0]
    if u == 1:
        return jnp.where(row == n - 1, 0.0, roll(v, n - 1, 0))
    return jnp.where(row == 0, 0.0, roll(v, 1, 0))


def band_block(w, start):
    lane = lax.broadcasted_iota(jnp.int32, (16, 128), 1)
    row = lax.broadcasted_iota(jnp.int32, (16, 128), 0)
    u = row // 8 - start - lane // 16
    return jnp.where(u == -1, w[0], jnp.where(u == 0, w[1], jnp.where(u == 1, w[2], 0.0))).astype(BF)


def band_sums(g):
    cell = lax.broadcasted_iota(jnp.int32, (16, 128), 1) // 8
    kept = [[jnp.zeros((16, 128), F32) for _ in range(3)] for _ in range(2)]
    for z in range(32):
        for half in range(2):
            if 16 * half - 1 <= z <= 16 * half + 16:
                t = cell + (16 * half - z)
                kept[half][z % 3] = jnp.where(t * t <= 1, g[z * 16:(z + 1) * 16, 128 * half:128 * (half + 1)], kept[half][z % 3])
    out = []
    for u in (-1, 0, 1):
        total = None
        for half in range(2):
            z = cell + (16 * half - u)
            r = (z + 3) % 3
            s = jnp.where(r == 0, kept[half][0], jnp.where(r == 1, kept[half][1], kept[half][2]))
            s = jnp.where((z >= 0) & (z < 32), s, 0.0)
            total = s if total is None else total + s
        out.append(total)
    return out


def lane_sums(v):
    same = (lax.broadcasted_iota(jnp.int32, (128, 128), 0) % 8 == lax.broadcasted_iota(jnp.int32, (128, 128), 1) % 8).astype(BF)
    total = None
    for _ in range(3):
        part = v.astype(BF)
        v = v - part.astype(F32)
        term = mm(part, same)
        total = term if total is None else total + term
    return total


def gates(hidden, back_active):
    gate = jax.nn.sigmoid(hidden)
    return hidden * gate, back_active * gate * (1.0 + hidden * (1.0 - gate))


def kernel(kspace_hbm, cotangent_hbm, mask, weight_in, weight_out, consistency, first_hbm, wide_hbm, rest_hbm,
           out, grad_in, grad_out,
           kspace, cotangent, first, wide, rest, wt, seml,
           a1, r1, s2, r2, planes, band, turned_band, zt, bh, send_p, recv_p, s3, r3, s4, r4, g_lanes, gr, ga, gs, gb, gt, gc,
           sem1, sem2, semh, semp, sem3, sem4, semg1, semg2, semg3):
    g = lax.axis_index("gy")
    j = lax.axis_index("gz")
    h, b = g // 16, g % 16
    m = h * 8 + j

    def dev1(p):
        return (lax.div(p, 8) * 16 + b, lax.rem(p, 8))

    def dev2(p):
        return (h * 16 + p, j)

    def at_x(p):
        member, place = member_of(p)
        return ((member // 8) * 16 + place, member % 8)

    x = plane_of(m, b)
    right = at_x((x + 1) % 256)
    left = at_x((x + 255) % 256)

    loads = [pltpu.make_async_copy(src, dst, seml.at[i]) for i, (src, dst) in enumerate((
        (first_hbm, first), (kspace_hbm, kspace), (cotangent_hbm, cotangent), (rest_hbm, rest), (wide_hbm, wide)))]
    for c in loads:
        c.start()
    barrier = pltpu.get_barrier_semaphore()

    for d in range(1, 16):
        pl.semaphore_signal(barrier, inc=1, device_id=dev1(lax.rem(m + d, 16)), device_id_type=pl.DeviceIdType.MESH)
        pl.semaphore_signal(barrier, inc=1, device_id=dev2(lax.rem(b + d, 16)), device_id_type=pl.DeviceIdType.MESH)
    pl.semaphore_signal(barrier, inc=1, device_id=right, device_id_type=pl.DeviceIdType.MESH)
    pl.semaphore_signal(barrier, inc=1, device_id=left, device_id_type=pl.DeviceIdType.MESH)

    qy, px, pbt = (first.at[256 * i:256 * (i + 1)] for i in range(3))
    wyt, mzt = (wide.at[256 * i:256 * (i + 1)] for i in range(2))
    wy, wy_low, mz, mz_low = (rest.at[512 * i:512 * (i + 1)] for i in range(4))
    pb, qyt, pxt = (rest.at[2048 + 256 * i:2304 + 256 * i] for i in range(3))

    def remote(src, dst, sems, i, device):
        return pltpu.make_async_remote_copy(
            src_ref=src, dst_ref=dst, send_sem=sems.at[0, i], recv_sem=sems.at[1, i],
            device_id=device, device_id_type=pl.DeviceIdType.MESH)

    def send_all(me, dev, src, dst, some, sems):
        for d in (8, 7, 9, 6, 10, 5, 11, 4, 12, 3, 13, 2, 14, 1, 15):
            p = lax.rem(me + d, 16)
            remote(src(p), dst(me), sems, 0, dev(p)).start()

    def wait_all(me, dev, src, dst, some, sems):
        remote(*some, sems, 0, dev(lax.rem(me + 1, 16))).wait_recv()

    def wait_sent(me, dev, src, dst, some, sems):
        remote(*some, sems, 0, dev(lax.rem(me + 1, 16))).wait_send()

    ex1 = [(m, dev1, lambda p, f=f: a1.at[f, p], lambda p, f=f: r1.at[f, p],
            (a1.at[f, 0:15], r1.at[f, 0:15]), sem1.at[f]) for f in range(2)]
    ex2 = [(b, dev2, lambda p, f=f: s2.at[f, p], lambda p, f=f: r2.at[f, p],
            (s2.at[f, 0:15], r2.at[f, 0:15]), sem2.at[f]) for f in range(2)]
    loads[0].wait()
    for f, field in enumerate((kspace, cotangent)):
        loads[1 + f].wait()
        rows = jnp.concatenate([field[:, z, :] for z in range(4)], axis=0)
        a1[f] = pack(rows, qy[...], px[...]).reshape(16, 16, 256)
        if f == 0:
            pl.semaphore_wait(barrier, 32)
        send_all(*ex1[f])
        r1[f, m] = a1[f, m]

    spread = (lax.broadcasted_iota(jnp.int32, (16, 128), 1) % 16 == lax.broadcasted_iota(jnp.int32, (16, 128), 0)).astype(BF)
    for f, w in enumerate((weight_in, weight_out)):
        wt[216 * f:216 * (f + 1), :] = mm(w[...].astype(F32).reshape(216, 16).astype(BF), spread)

    def build(t, carry):
        f, uy, ux = t // 9, t % 9 // 3, t % 3
        w = []
        for uz in range(3):
            k = uy * 9 + uz * 3 + ux
            k = k + f * (53 - 2 * k)
            block = wt[pl.ds(pl.multiple_of(k * 8, 8), 8), :]
            w.append(jnp.concatenate([block, block], axis=0))
        at = [band_block(w, -2 * i) for i in range(4)]
        before, after = band_block(w, -8), band_block(w, 2)
        zero = jnp.zeros((16, 128), BF)
        for pair in range(16):
            own = pair // 4
            cells = [zero] * 4
            cells[own] = at[pair % 4]
            if pair % 4 == 0 and own > 0:
                cells[own - 1] = before
            if pair % 4 == 3 and own < 3:
                cells[own + 1] = after
            rows_at = pl.multiple_of(t * 256 + pair * 16, 16)
            band[pl.ds(rows_at, 16), :] = jnp.concatenate(cells, axis=1)
        return carry

    lax.fori_loop(0, 18, build, 0)

    def turn(t, carry):
        rows_at = pl.multiple_of(t * 256, 256)
        turned_at = pl.multiple_of(t // 3 * 512, 512)
        turned_band[t % 3, pl.ds(turned_at, 512), :] = band[pl.ds(rows_at, 256), :].T
        return carry

    lax.fori_loop(0, 9, turn, 0)

    def halo_copies(f):
        return (remote(planes.at[f, 1], planes.at[f, 0], semh, f, right),
                remote(planes.at[f, 1], planes.at[f, 2], semh, 2 + f, left))

    for f in range(2):
        wait_all(*ex1[f])
        parts = [jnp.concatenate([r1[f, k], r1[f, 8 + k]], axis=0).astype(F32) for k in range(8)]
        whole = jnp.concatenate(swap_blocks(parts), axis=0).astype(BF)
        s2[f] = mm(pbt[...], whole).astype(BF).reshape(16, 16, 256)
        send_all(*ex2[f])
        r2[f, b] = s2[f, b]

    loads[3].wait()
    loads[4].wait()
    for f in range(2):
        wait_sent(*ex1[f])
    for f in range(2):
        wait_all(*ex2[f])
        v = to_volume(r2[f].reshape(256, 256), (wy[...], wy_low[...]), (mz[...], mz_low[...]))
        planes[f, 1] = (v if f == 0 else -v).astype(BF)
        for c in halo_copies(f):
            c.start()

    for f in range(2):
        wait_sent(*ex2[f])
    convolved = []
    for f in range(2):
        for c in halo_copies(f):
            c.wait()

        @pl.when(x == 0)
        def _():
            planes[f, 0] = jnp.zeros((256, 256), BF)

        @pl.when(x == 255)
        def _():
            planes[f, 2] = jnp.zeros((256, 256), BF)

        cat = jnp.concatenate([planes[f, ux] for ux in range(3)], axis=1)
        total = None
        for uy in (-1, 0, 1):
            row = f * 2304 + (uy + 1) * 768
            v = shifted(mm(cat, band[row:row + 768, :]), uy)
            total = v if total is None else total + v
        convolved.append(total)

    active, back_hidden = gates(*convolved)
    for uy in (-1, 0, 1):
        bh[:, (uy + 1) * 512:(uy + 2) * 512] = shifted(back_hidden, -uy).astype(BF)

    def share(side):
        return mm(bh[...], turned_band[side])

    away = x % 2
    near = 1 - away
    share_copies = []
    for i, side in enumerate((away, near)):
        send_p[i] = share(2 * side).astype(BF)
        c = remote(send_p.at[i], recv_p.at[i], semp, i, at_x((x + 255 + 2 * side) % 256))
        c.start()
        share_copies.append(c)
    own = share(1)

    lane = lax.broadcasted_iota(jnp.int32, (512, 256), 1)
    for f, v in enumerate((back_hidden, active)):
        v = v.T
        zt[f, 0] = jnp.where(lane == 255, 0.0, roll(v, 255, 1)).astype(BF)
        zt[f, 1] = v.astype(BF)
        zt[f, 2] = jnp.where(lane == 0, 0.0, roll(v, 1, 1)).astype(BF)
    for t in range(18):
        gm = mm(zt[t // 9, t % 9 // 3], planes[t // 9, t % 3])
        for u, v in enumerate(band_sums(gm)):
            k = t * 3 + u
            g_lanes[k * 16:(k + 1) * 16, :] = v
    sums = lane_sums(g_lanes[...])
    slot = lax.broadcasted_iota(jnp.int32, (16, 128), 1) // 8
    for tile in range(8):
        v = jnp.zeros((16, 128), F32)
        for at in range(7):
            k = 7 * tile + at
            if k < 54:
                v = jnp.where(slot == at, sums[k * 16:(k + 1) * 16], v)
        gr[2 * tile] = v[:8]
        gr[2 * tile + 1] = v[8:]
    exg1 = (m, dev1, lambda p: gr.at[p], lambda p: ga.at[p], (gr.at[0:15], ga.at[0:15]), semg1)
    send_all(*exg1)
    ga[m] = gr[m]

    for c in share_copies:
        c.wait()
    inside = jnp.where((x > 0) & (x < 255), 1.0, 0.0)
    back_image = own + recv_p[0].astype(F32) * inside + recv_p[1].astype(F32)

    s3[...] = from_volume(back_image, wyt[...], mzt[...]).reshape(16, 16, 256)
    ex3 = (b, dev2, lambda p: s3.at[p], lambda p: r3.at[p], (s3.at[0:15], r3.at[0:15]), sem3)
    send_all(*ex3)
    r3[b] = s3[b]

    wait_all(*exg1)
    gs[...] = jnp.broadcast_to(jnp.sum(ga[...], axis=0, keepdims=True), (16, 8, 128))
    exg2 = (b, dev2, lambda p: gs.at[p], lambda p: gb.at[p], (gs.at[0:15], gb.at[0:15]), semg2)
    send_all(*exg2)
    gb[b] = gs[b]

    wait_all(*ex3)
    rows = mm(pb[...], r3[...].reshape(256, 256))
    parts = swap_blocks([rows[k * 32:(k + 1) * 32] for k in range(8)])
    for k in range(8):
        v = parts[k].astype(BF)
        s4[k] = v[:16]
        s4[8 + k] = v[16:]
    ex4 = (m, dev1, lambda p: s4.at[p], lambda p: r4.at[p], (s4.at[0:15], r4.at[0:15]), sem4)
    send_all(*ex4)
    r4[m] = s4[m]

    wait_all(*exg2)
    gt[...] = jnp.broadcast_to(jnp.sum(gb[...], axis=0, keepdims=True), (16, 8, 128))
    exg3 = (m, dev1, lambda p: gt.at[p], lambda p: gc.at[p], (gt.at[0:15], gc.at[0:15]), semg3)
    send_all(*exg3)
    gc[m] = gt[m]

    for e in (ex3, exg1, exg2):
        wait_sent(*e)
    wait_all(*ex4)
    spectrum = unpack(r4[...].reshape(256, 256), qyt[...], pxt[...])
    factor = mask[...].astype(F32)
    eye = lax.broadcasted_iota(jnp.int32, (8, 8), 0) == lax.broadcasted_iota(jnp.int32, (8, 8), 1)
    for z in range(4):
        rows = cotangent[:, z, :]
        sampled = jnp.sum(jnp.where(eye, factor[z:z + 1], 0.0), axis=1, keepdims=True) * consistency[0]
        scaled = (rows.reshape(8, 8, 256) * sampled[None]).reshape(64, 256)
        out[:, z, :] = rows - scaled + spectrum[z * 64:(z + 1) * 64]

    for e in (ex4, exg3):
        wait_sent(*e)
    wait_all(*exg3)
    turned = gc[...].reshape(128, 128).T
    for t in range(8):
        at_front = turned if t == 0 else roll(turned, 128 - 16 * t, 1)
        for slot_at in range(7):
            k = 7 * t + slot_at
            if k < 54:
                f, uy, ux, uz = k // 27, k // 9 % 3, k // 3 % 3, k % 3
                n = uy * 9 + uz * 3 + ux
                block = at_front[slot_at * 8:slot_at * 8 + 8, :16]
                if f == 0:
                    grad_in[n] = block
                else:
                    grad_out[26 - n] = block


def local(kspace, cotangent, weight_in, weight_out, consistency_weight, sampling_mask):
    w_in = weight_in.transpose(2, 3, 4, 1, 0).reshape(27, 8, 16)
    w_out = weight_out.transpose(2, 3, 4, 0, 1).reshape(27, 8, 16)
    vmem = pl.BlockSpec(memory_space=pltpu.VMEM)
    hbm = pl.BlockSpec(memory_space=pltpu.HBM)

    def scratch(*shape, kind=BF):
        return pltpu.VMEM(shape, kind)

    def sems(n):
        return pltpu.SemaphoreType.DMA((2, n))

    grad_shape = jax.ShapeDtypeStruct((27, 8, 16), F32)
    out, grad_in, grad_out = pl.pallas_call(
        kernel,
        out_shape=(pltpu.VMEM((64, 4, 256), F32), pltpu.VMEM((27, 8, 16), F32), pltpu.VMEM((27, 8, 16), F32)),
        in_specs=[hbm, hbm, vmem, vmem, vmem, pl.BlockSpec(memory_space=pltpu.SMEM), hbm, hbm, hbm],
        out_specs=(vmem, vmem, vmem),
        scratch_shapes=[
            scratch(64, 4, 256, kind=F32), scratch(64, 4, 256, kind=F32),
            scratch(768, 256), scratch(512, 512), scratch(2816, 256), scratch(432, 128, kind=F32),
            pltpu.SemaphoreType.DMA((5,)),
            scratch(2, 16, 16, 256), scratch(2, 16, 16, 256), scratch(2, 16, 16, 256), scratch(2, 16, 16, 256),
            scratch(2, 3, 256, 256), scratch(4608, 512), scratch(3, 1536, 256), scratch(2, 3, 512, 256), scratch(256, 1536),
            scratch(2, 256, 256), scratch(2, 256, 256),
            scratch(16, 16, 256), scratch(16, 16, 256),
            scratch(16, 16, 256), scratch(16, 16, 256),
            scratch(864, 128, kind=F32), *[scratch(16, 8, 128, kind=F32) for _ in range(6)],
            pltpu.SemaphoreType.DMA((2, 2, 1)), pltpu.SemaphoreType.DMA((2, 2, 1)), sems(4), sems(2), sems(1), sems(1), sems(1), sems(1), sems(1),
        ],
        compiler_params=pltpu.CompilerParams(
            collective_id=0, has_side_effects=True, vmem_limit_bytes=60 * 1024 * 1024),
        name="cascade",
    )(kspace.reshape(64, 4, 256), cotangent.reshape(64, 4, 256), sampling_mask.T, w_in, w_out, consistency_weight, *map(jnp.asarray, tables()))
    scale = 1.0 / math.sqrt(2097152)
    grad_in = (grad_in * scale).reshape(3, 3, 3, 8, 16).transpose(4, 3, 0, 1, 2)
    grad_out = (grad_out * scale).reshape(3, 3, 3, 8, 16).transpose(3, 4, 0, 1, 2)
    return out.reshape(kspace.shape), grad_in, grad_out


def solution(mesh):
    placed = P(None, None, "gy", "gz", None)
    return jax.shard_map(
        local,
        mesh=mesh,
        in_specs=(placed, placed, P(), P(), P(), P("gy", "gz")),
        out_specs=(placed, P(), P()),
        check_vma=False,
    )
```
